32 devices in a mesh: grp: 4 (over y, x), dev: 8 (over z, core).
Axes of the slice: x: 2, y: 2, z: 4, core: 2. Of those that a mesh axis runs over, the one named last changes fastest.
Arguments:
- queries: bfloat16 [32, 3072], P(('grp', 'dev')), may hold values from -480 to 480
- cached_key_rows: bfloat16 [32, 512, 512], P(('grp', 'dev')), may hold values from -6 to 6
- cached_value_rows: bfloat16 [32, 512, 512], P(('grp', 'dev')), may hold values from -6 to 6
- incoming_keys: bfloat16 [32, 512], P(('grp', 'dev')), may hold values from -6 to 6
- incoming_values: bfloat16 [32, 512], P(('grp', 'dev')), may hold values from -6 to 6
- lengths: int32 [16], P('grp'), may hold values from 64 to 512, as said below
- residual: bfloat16 [16, 6144], P('grp'), may hold values from -6 to 6
- norm_gain: float32 [6144], replicated, may hold values from 0.25 to 1.75
- expert_ids: int32 [16, 2], P('grp'), may hold values from 0 to 7, all different within a row; in each aligned block of 4 rows (0 to 3, 4 to 7, ...) at most 4 rows name the same one
- route_logits: float32 [16, 2], P('grp'), may hold values from -6 to 6
- w_gate: bfloat16 [6144, 65536], P(None, ('dev', 'grp')), may hold values from -0.078125 to 0.078125
- w_up: bfloat16 [6144, 65536], P(None, ('dev', 'grp')), may hold values from -0.078125 to 0.078125
- w_down: bfloat16 [65536, 6144], P(('dev', 'grp')), may hold values from -0.0625 to 0.0625
Outputs:
- moe_out: bfloat16 [16, 6144], P('grp', 'dev')
The draws below stay inside these ranges and needn't reach their ends.
Inputs may be any that keep to these rules, and one draw needn't show every extreme that they name: `lengths`: A sequence has at least 64 live positions; some sequence has exactly 512. `expert_ids`: each token names 2 different experts; among the tokens of one group (4 aligned rows) no expert is named more than 4 times, a bound that some block reaches.
All inputs are finite; a program needn't handle non-finite values.
Results may differ from the reference program's by a relative error of at most 0.007.
Values may be sent and summed in bfloat16 or wider, within the bound.
No kernel may reach another device: no remote copies, remote signals or barrier semaphores. Data moves between devices by JAX's collectives and lax.ppermute only.
A program may use at most 192 MiB of HBM per device.

```python
import math
import jax
import jax.numpy as jnp
import numpy as np
from jax import lax

D = 6144
QUERY_HEADS = 48
KEY_VALUE_HEADS = 8
HEAD_SIZE = 128
E = 8
FF = 8192
TOPK = 2
SHARING_DEVICES = 2
CACHED_POSITIONS = 512
TOK_GRP = 4
TOTAL_SEQUENCES = 16
ROWCAP = 4
N_GRP = 4


def draw_queries(key, part):
    first_key = jax.random.fold_in(key, 0)
    values = jnp.clip(jax.random.normal(first_key, (TOTAL_SEQUENCES * SHARING_DEVICES, QUERY_HEADS // SHARING_DEVICES, HEAD_SIZE), jnp.float32), -6.0, 6.0)
    return values.reshape(TOTAL_SEQUENCES * SHARING_DEVICES, D // SHARING_DEVICES).astype(jnp.bfloat16)


def draw_lengths(key, part):
    first_key, second_key = jax.random.split(key)
    drawn = jax.random.randint(first_key, (TOTAL_SEQUENCES,), CACHED_POSITIONS // 8, CACHED_POSITIONS + 1, jnp.int32)
    longest = jax.random.randint(second_key, (), 0, TOTAL_SEQUENCES, jnp.int32)
    return jnp.where(jnp.arange(TOTAL_SEQUENCES, dtype=jnp.int32) == longest, CACHED_POSITIONS, drawn).astype(jnp.int32)


def levels(key, shape, shards, low, top_value):
    def one(dim, shards_of):
        draws = jax.random.uniform(jax.random.fold_in(jax.random.fold_in(key, 6), dim), (shards_of,), jnp.float32, low / len(shards), top_value / len(shards))
        return jnp.repeat(jnp.exp(draws), shape[dim] // shards_of).reshape((-1,) + (1,) * (len(shape) - dim - 1))

    gain = one(*shards[0])
    for cut in shards[1:]:
        gain = gain * one(*cut)
    return gain


def routed_block(own_key, own, number, rows, number_of, top, reach, skew):
    sequence = jax.random.permutation(own_key, number_of)
    crowded, usual = portions_of(number_of, rows * top, reach, skew, True), portions_of(number_of, rows * top, reach, skew, False)
    places = jnp.arange(number_of)

    def named(tallies, turn):
        used = int((tallies > 0).sum())
        fixed = max(1, used // 4)
        shifted = fixed + (places - fixed + turn * (used - fixed)) % max(1, number_of - fixed)
        return jnp.zeros((number_of,), jnp.int32).at[sequence[jnp.where(places < fixed, places, shifted)]].set(jnp.asarray(tallies, jnp.int32))

    tallies = jnp.where(number % 4 == 0, named(crowded, number // 4), named(usual, number - number // 4 - 1))
    mixed = jax.random.permutation(jax.random.fold_in(own, 3), number_of)
    source_of, taker = mixed[0:number_of // 2 * 2:2], mixed[1:number_of // 2 * 2:2]
    margin = jnp.minimum(tallies[source_of] - 1, reach - tallies[taker]) // 2
    margin = jnp.where((source_of == sequence[0]) | (taker == sequence[0]) | (tallies[taker] == 0), 0, jnp.maximum(margin, 0))
    shifted = jax.random.randint(jax.random.fold_in(own, 4), (number_of // 2,), 0, 1 << 20) % (margin + 1)
    tallies = tallies.at[source_of].add(-shifted).at[taker].add(shifted)
    items = jnp.searchsorted(jnp.cumsum(tallies), jnp.arange(rows * top), side="right").astype(jnp.int32)
    grid = items.reshape(top, rows).T
    grid = grid[jax.random.permutation(jax.random.fold_in(own, 1), rows)]
    turn = jax.random.randint(jax.random.fold_in(own, 2), (rows, 1), 0, top)
    return jnp.take_along_axis(grid, (jnp.arange(top)[None, :] + turn) % top, axis=1)


def portions_of(number_of, total, most, lean, full):
    portions = [(1 << 20) // math.isqrt(rank ** lean) + 1 for rank in range(1, number_of + 1)]
    largest = most if full else min(most, max(-(-total // number_of), total * portions[0] // sum(portions)))
    least = 1 if total - largest >= number_of - 1 else 0
    given, surplus = [largest] + [least] * (number_of - 1), total - largest - least * (number_of - 1)
    while surplus > 0:
        free = [i for i in range(1, number_of) if given[i] < largest] or [i for i in range(1, number_of) if given[i] < most]
        mass, budget = sum([portions[i] for i in free]), surplus
        for i in free:
            extra = min(most - given[i], max(1, budget * portions[i] // mass), surplus)
            given[i] = given[i] + extra
            surplus = surplus - extra
    return np.array(given)


def scatter_about(own_key, dims, deviation, most, cuts=(), kind=jnp.bfloat16):
    gain = levels(own_key, dims, cuts, -0.22, 0.18) if cuts else 1.0
    result = jax.random.normal(own_key, dims, jnp.float32) * deviation * gain
    return jnp.minimum(jnp.maximum(result, -most), most).astype(kind)


def setup_inputs(seed: int = 0) -> dict:
    key_list = jax.random.split(jax.random.key(seed), 14)
    queries = draw_queries(jax.random.fold_in(key_list[13], 71), 0)
    cached_key_rows = scatter_about(key_list[1], (TOTAL_SEQUENCES * SHARING_DEVICES, CACHED_POSITIONS, KEY_VALUE_HEADS // SHARING_DEVICES * HEAD_SIZE), 1.0, 6.0, ((0, 32),))
    cached_value_rows = scatter_about(key_list[2], (TOTAL_SEQUENCES * SHARING_DEVICES, CACHED_POSITIONS, KEY_VALUE_HEADS // SHARING_DEVICES * HEAD_SIZE), 1.0, 6.0, ((0, 32),))
    incoming_keys = scatter_about(key_list[3], (TOTAL_SEQUENCES * SHARING_DEVICES, KEY_VALUE_HEADS // SHARING_DEVICES * HEAD_SIZE), 1.0, 6.0, ((0, 32),))
    incoming_values = scatter_about(key_list[4], (TOTAL_SEQUENCES * SHARING_DEVICES, KEY_VALUE_HEADS // SHARING_DEVICES * HEAD_SIZE), 1.0, 6.0, ((0, 32),))
    lengths = draw_lengths(jax.random.fold_in(key_list[13], 71), 0)
    residual = scatter_about(key_list[6], (TOTAL_SEQUENCES, D), 1.0, 6.0, ((0, 4),))
    norm_gain = jnp.clip(1.0 + 0.15 * jax.random.normal(key_list[7], (D,), jnp.float32), 0.25, 1.75)
    expert_ids_keys = jax.random.split(jax.random.fold_in(key_list[8], 1), TOTAL_SEQUENCES // TOK_GRP)
    expert_ids_turns = jax.random.permutation(jax.random.fold_in(key_list[8], 3), TOTAL_SEQUENCES // TOK_GRP)
    expert_ids = jax.vmap(lambda own, number: routed_block(jax.random.fold_in(key_list[8], 2), own, number, TOK_GRP, E, TOPK, ROWCAP, 2))(expert_ids_keys, expert_ids_turns).reshape((TOTAL_SEQUENCES, TOPK))
    route_logits = scatter_about(key_list[9], (TOTAL_SEQUENCES, TOPK), 1.5, 6.0, ((0, 4),), jnp.float32)
    w_gate = scatter_about(key_list[10], (D, E * FF), D ** -0.5, 0.078125, ((1, 32),))
    w_up = scatter_about(key_list[11], (D, E * FF), D ** -0.5, 0.078125, ((1, 32),))
    w_down = scatter_about(key_list[12], (E * FF, D), FF ** -0.5, 0.0625, ((0, 32),))
    return {"queries": queries, "cached_key_rows": cached_key_rows, "cached_value_rows": cached_value_rows, "incoming_keys": incoming_keys, "incoming_values": incoming_values, "lengths": lengths, "residual": residual, "norm_gain": norm_gain, "expert_ids": expert_ids, "route_logits": route_logits, "w_gate": w_gate, "w_up": w_up, "w_down": w_down}


def slot_matrix(id_rows, prob_rows, expert, slot_cap):
    matched = (id_rows == expert).astype(jnp.int32).reshape(-1)
    position = (jnp.cumsum(matched) - matched).astype(jnp.int32)
    slot_hit = (position[None, :] == jnp.arange(slot_cap, dtype=jnp.int32)[:, None]) & (matched[None, :] > 0)
    slot_hit = slot_hit.astype(jnp.float32).reshape(slot_cap, id_rows.shape[0], id_rows.shape[1])
    return (lax.optimization_barrier(jnp.sum(slot_hit, axis=2)), lax.optimization_barrier(jnp.sum(slot_hit * prob_rows[None], axis=(1, 2))))

def attend_row(packed):
    query_vec, key_rows, value_rows, key_fresh, value_fresh, length_row = packed
    head_local = key_rows.shape[1] // HEAD_SIZE
    query_group_width = QUERY_HEADS // KEY_VALUE_HEADS
    score_scale = HEAD_SIZE ** (-0.5)
    query_mat = query_vec.astype(jnp.float32).reshape(head_local, query_group_width, HEAD_SIZE)
    key_mat = key_rows.astype(jnp.float32).reshape(CACHED_POSITIONS, head_local, HEAD_SIZE)
    value_mat = value_rows.astype(jnp.float32).reshape(CACHED_POSITIONS, head_local, HEAD_SIZE)
    score_all = jnp.einsum('hgd,thd->hgt', query_mat, key_mat) * score_scale
    mask_live = jnp.arange(CACHED_POSITIONS, dtype=jnp.int32) < length_row
    score_all = jnp.where(mask_live[None, None, :], score_all, -1e+30)
    new_score = jnp.einsum('hgd,hd->hg', query_mat, key_fresh.astype(jnp.float32).reshape(head_local, HEAD_SIZE)) * score_scale
    row_max = jnp.maximum(lax.optimization_barrier(jnp.max(score_all, axis=-1)), new_score)
    exp_all = jnp.exp(score_all - row_max[..., None])
    exp_new = jnp.exp(new_score - row_max)
    denom_all = lax.optimization_barrier(jnp.sum(exp_all, axis=-1)) + exp_new
    attn_weights = lax.optimization_barrier((exp_all / denom_all[..., None]).astype(jnp.bfloat16)).astype(jnp.float32)
    weight_new = lax.optimization_barrier((exp_new / denom_all).astype(jnp.bfloat16)).astype(jnp.float32)
    mixed_out = jnp.einsum('hgt,thd->hgd', attn_weights, value_mat)
    mixed_out = mixed_out + weight_new[..., None] * value_fresh.astype(jnp.float32).reshape(head_local, 1, HEAD_SIZE)
    return mixed_out.reshape(-1).astype(jnp.bfloat16)

def reference(queries, cached_key_rows, cached_value_rows, incoming_keys, incoming_values, lengths, residual, norm_gain, expert_ids, route_logits, w_gate, w_up, w_down):
    row_lengths = jnp.repeat(lengths, SHARING_DEVICES).astype(jnp.int32)
    attended = lax.map(attend_row, (queries, cached_key_rows, cached_value_rows, incoming_keys, incoming_values, row_lengths))
    heads_all = attended.reshape(TOTAL_SEQUENCES, D)
    summed = residual.astype(jnp.float32) + heads_all.astype(jnp.float32)
    normed = (summed * lax.rsqrt(lax.optimization_barrier(jnp.mean(summed * summed, axis=-1, keepdims=True)) + 1e-05) * norm_gain).astype(jnp.bfloat16)
    route_probs = jax.nn.softmax(route_logits.astype(jnp.float32), axis=-1)
    group_ids = expert_ids.reshape(N_GRP, TOK_GRP, TOPK)
    group_probs = route_probs.reshape(N_GRP, TOK_GRP, TOPK)
    group_rows = normed.astype(jnp.float32).reshape(N_GRP, TOK_GRP, D)
    total_out = jnp.zeros((N_GRP, TOK_GRP, D), jnp.float32)
    for expert in range(E):

        def one_group(id_rows, prob_rows):
            return slot_matrix(id_rows, prob_rows, expert, ROWCAP)
        select_all, slot_weight = jax.vmap(one_group)(group_ids, group_probs)
        picked = jnp.einsum('gct,gtd->gcd', select_all, group_rows).astype(jnp.bfloat16).reshape(N_GRP * ROWCAP, D)
        gate_out = jnp.dot(picked, w_gate[:, expert * FF:(expert + 1) * FF], preferred_element_type=jnp.float32)
        up_out = jnp.dot(picked, w_up[:, expert * FF:(expert + 1) * FF], preferred_element_type=jnp.float32)
        hidden = (jax.nn.silu(gate_out) * up_out).astype(jnp.bfloat16)
        expert_out = jnp.dot(hidden, w_down[expert * FF:(expert + 1) * FF], preferred_element_type=jnp.float32)
        expert_out = expert_out.reshape(N_GRP, ROWCAP, D)
        total_out = total_out + jnp.einsum('gct,gc,gcd->gtd', select_all, slot_weight, expert_out, precision=lax.Precision.HIGHEST)
    return total_out.reshape(TOTAL_SEQUENCES, D).astype(jnp.bfloat16)
```

```python
import functools

import jax
import jax.numpy as jnp
from jax import lax
from jax.experimental import pallas as pl
from jax.experimental.pallas import tpu as pltpu
from jax.sharding import PartitionSpec as P

QUERY_HEADS = 48
KEY_VALUE_HEADS = 8
HEAD_SIZE = 128
E = 8
SHARING_DEVICES = 2
GROUP_WIDTH = QUERY_HEADS // KEY_VALUE_HEADS
LOCAL_HEADS = QUERY_HEADS // SHARING_DEVICES
MIB = 2**20
VMEM = pl.BlockSpec(memory_space=pltpu.VMEM)
SMEM = pl.BlockSpec(memory_space=pltpu.SMEM)
ANY = pl.BlockSpec(memory_space=pl.ANY)


def head_rows(row):
    heads = row.shape[1] // HEAD_SIZE
    return jnp.concatenate(
        [row[:, j * HEAD_SIZE : (j + 1) * HEAD_SIZE] for j in range(heads)], axis=0
    )


def attend_kernel(
    lengths, queries, key_rows, value_rows, new_keys, new_values, residual, out
):
    position = lax.axis_index("dev")
    sequence = lax.div(position, SHARING_DEVICES)
    half = lax.rem(position, SHARING_DEVICES)
    heads, cache_len = LOCAL_HEADS, key_rows.shape[1]
    width = key_rows.shape[2]
    kv_heads = width // HEAD_SIZE
    scale = HEAD_SIZE ** (-0.5)
    query = head_rows(queries[...].astype(jnp.float32))
    owner = lax.broadcasted_iota(jnp.int32, (heads, HEAD_SIZE), 0) // GROUP_WIDTH
    blocks = [jnp.where(owner == b, query, 0.0) for b in range(kv_heads)]
    spread = jnp.concatenate(blocks, axis=1)
    scores = (
        lax.dot_general(
            spread.astype(jnp.bfloat16),
            key_rows[0],
            (((1,), (1,)), ((), ())),
            preferred_element_type=jnp.float32,
        )
        * scale
    )
    places = lax.broadcasted_iota(jnp.int32, (heads, cache_len), 1)
    scores = jnp.where(places < lengths[sequence], scores, -1e30)
    new_score = (
        jnp.sum(spread * new_keys[...].astype(jnp.float32), axis=1, keepdims=True) * scale
    )
    row_max = jnp.maximum(jnp.max(scores, axis=1, keepdims=True), new_score)
    exp_all = jnp.exp(scores - row_max)
    exp_new = jnp.exp(new_score - row_max)
    denom = jnp.sum(exp_all, axis=1, keepdims=True) + exp_new
    weights = (exp_all / denom).astype(jnp.bfloat16)
    weight_new = (exp_new / denom).astype(jnp.bfloat16).astype(jnp.float32)
    mixed = jnp.dot(weights, value_rows[0], preferred_element_type=jnp.float32)
    mixed = mixed + weight_new * new_values[...].astype(jnp.float32)
    attended = jnp.zeros((heads, HEAD_SIZE), jnp.float32)
    for b in range(kv_heads):
        attended = jnp.where(
            owner == b, mixed[:, b * HEAD_SIZE : (b + 1) * HEAD_SIZE], attended
        )
    attended = attended.astype(jnp.bfloat16).astype(jnp.float32)
    columns = heads * HEAD_SIZE
    mine = residual[:, pl.ds(pl.multiple_of(half * columns, HEAD_SIZE), columns)].astype(jnp.float32)
    rows = lax.broadcasted_iota(jnp.int32, mine.shape, 0)
    mine = jnp.sum(jnp.where(rows == sequence, mine, 0.0), axis=0, keepdims=True)
    summed = (attended + head_rows(mine)).astype(jnp.bfloat16)
    out[...] = jnp.broadcast_to(summed[None], out.shape)


def attend(lengths, queries, key_rows, value_rows, new_keys, new_values, residual, devices):
    return pl.pallas_call(
        attend_kernel,
        out_shape=jax.ShapeDtypeStruct((devices, LOCAL_HEADS, HEAD_SIZE), jnp.bfloat16),
        in_specs=[SMEM] + [VMEM] * 6,
        out_specs=VMEM,
        compiler_params=pltpu.CompilerParams(vmem_limit_bytes=24 * MIB),
        name="attend",
    )(lengths, queries, key_rows, value_rows, new_keys, new_values, residual)


def experts_kernel(
    parts, gain, w_gate, w_up, w_down, out,
    flat, normed, hidden, gate_buf, up_buf, down_buf, gate_sem, up_sem, down_sem,
):
    devices = parts.shape[0]
    tokens, width = normed.shape
    ring, _, tile = gate_buf.shape
    tiles = w_gate.shape[1] // tile
    columns = out.shape[2]
    slices = w_down.shape[1] // columns
    down_ring = down_buf.shape[0]

    def copies(n):
        at = pl.ds(pl.multiple_of(n * tile, tile), tile)
        slot = lax.rem(n, ring)
        return (
            pltpu.make_async_copy(w_gate.at[:, at], gate_buf.at[slot], gate_sem.at[slot]),
            pltpu.make_async_copy(w_up.at[:, at], up_buf.at[slot], up_sem.at[slot]),
        )

    def down_copy(n):
        at = pl.ds(pl.multiple_of(n * columns, HEAD_SIZE), columns)
        slot = lax.rem(n, down_ring)
        return pltpu.make_async_copy(w_down.at[:, at], down_buf.at[slot], down_sem.at[slot])

    for n in range(min(ring, tiles)):
        for copy in copies(n):
            copy.start()
    for n in range(min(down_ring, slices)):
        down_copy(n).start()

    flat[...] = parts[...].astype(jnp.float32).reshape(flat.shape)
    heads = width // HEAD_SIZE
    square = jnp.zeros((tokens, HEAD_SIZE), jnp.float32)
    for j in range(heads):
        piece = flat[pl.ds(j, tokens, stride=heads), :]
        square = square + piece * piece
    mean = jnp.sum(square, axis=1, keepdims=True) * (1.0 / width)
    inverse = lax.rsqrt(mean + 1e-05)
    for j in range(heads):
        piece = flat[pl.ds(j, tokens, stride=heads), :]
        normed[:, j * HEAD_SIZE : (j + 1) * HEAD_SIZE] = (
            piece * inverse * gain[j : j + 1, :]
        ).astype(jnp.bfloat16)

    def gate_step(n, carry):
        slot = lax.rem(n, ring)
        for copy in copies(n):
            copy.wait()
        gate = jnp.dot(normed[...], gate_buf[slot], preferred_element_type=jnp.float32)
        up = jnp.dot(normed[...], up_buf[slot], preferred_element_type=jnp.float32)
        at = pl.ds(pl.multiple_of(n * tile, tile), tile)
        hidden[:, at] = (gate / (1.0 + jnp.exp(-gate)) * up).astype(jnp.bfloat16)

        @pl.when(n + ring < tiles)
        def _():
            for copy in copies(n + ring):
                copy.start()

        return carry

    lax.fori_loop(0, tiles, gate_step, 0)

    group_rows = out.shape[1]

    def down_step(n, carry):
        slot = lax.rem(n, down_ring)
        down_copy(n).wait()
        part = jnp.dot(hidden[...], down_buf[slot], preferred_element_type=jnp.float32)
        for g in range(tokens // group_rows):
            out[g * slices + n] = part[g * group_rows : (g + 1) * group_rows].astype(out.dtype)

        @pl.when(n + down_ring < slices)
        def _():
            down_copy(n + down_ring).start()

        return carry

    lax.fori_loop(0, slices, down_step, 0)


def experts(parts, gain, w_gate, w_up, w_down, group_rows, dev_count):
    devices = parts.shape[0]
    width, local_hidden = w_gate.shape
    tokens = devices * LOCAL_HEADS * HEAD_SIZE // width
    tile, ring, down_ring = 512, 2, 6
    columns = width // dev_count
    return pl.pallas_call(
        experts_kernel,
        out_shape=jax.ShapeDtypeStruct((devices, group_rows, columns), jnp.bfloat16),
        in_specs=[VMEM, VMEM, ANY, ANY, ANY],
        out_specs=VMEM,
        scratch_shapes=[
            pltpu.VMEM((devices * LOCAL_HEADS, HEAD_SIZE), jnp.float32),
            pltpu.VMEM((tokens, width), jnp.bfloat16),
            pltpu.VMEM((tokens, local_hidden), jnp.bfloat16),
            pltpu.VMEM((ring, width, tile), jnp.bfloat16),
            pltpu.VMEM((ring, width, tile), jnp.bfloat16),
            pltpu.VMEM((down_ring, local_hidden, columns), jnp.bfloat16),
            pltpu.SemaphoreType.DMA((ring,)),
            pltpu.SemaphoreType.DMA((ring,)),
            pltpu.SemaphoreType.DMA((down_ring,)),
        ],
        compiler_params=pltpu.CompilerParams(vmem_limit_bytes=56 * MIB),
        name="experts",
    )(parts, gain.reshape(width // HEAD_SIZE, HEAD_SIZE), w_gate, w_up, w_down)


def experts_plain(parts, gain, w_gate, w_up, w_down, group_rows, dev_count):
    devices = parts.shape[0]
    width = w_gate.shape[0]
    summed = parts.reshape(-1, width).astype(jnp.float32)
    normed = (
        summed * lax.rsqrt(jnp.mean(summed * summed, axis=-1, keepdims=True) + 1e-05) * gain
    ).astype(jnp.bfloat16)
    gate = jnp.dot(normed, w_gate, preferred_element_type=jnp.float32)
    up = jnp.dot(normed, w_up, preferred_element_type=jnp.float32)
    hidden = (jax.nn.silu(gate) * up).astype(jnp.bfloat16)
    part = jnp.dot(hidden, w_down, preferred_element_type=jnp.float32).astype(jnp.bfloat16)
    part = part.reshape(-1, group_rows, dev_count, width // dev_count)
    return part.transpose(0, 2, 1, 3).reshape(devices, group_rows, -1)


def combine_kernel(per_expert, dev_count, parts, ids, logits, out):
    shards = parts.shape[0] // dev_count
    logit = logits[...]
    top = jnp.max(logit, axis=1, keepdims=True)
    raised = jnp.exp(logit - top)
    probs = raised / jnp.sum(raised, axis=1, keepdims=True)
    chosen = ids[...]
    total = jnp.zeros(out.shape, jnp.float32)
    for e in range(E):
        weight = jnp.sum(jnp.where(chosen == e, probs, 0.0), axis=1, keepdims=True)
        here = jnp.zeros(out.shape, jnp.float32)
        for g in range(shards):
            for c in range(per_expert):
                here = here + parts[g * dev_count + e * per_expert + c].astype(jnp.float32)
        total = total + weight * here
    out[...] = total.astype(out.dtype)


def combine(parts, ids, logits, dev_count):
    return pl.pallas_call(
        functools.partial(combine_kernel, dev_count // E, dev_count),
        out_shape=jax.ShapeDtypeStruct(parts.shape[1:], jnp.bfloat16),
        in_specs=[VMEM] * 3,
        out_specs=VMEM,
        compiler_params=pltpu.CompilerParams(vmem_limit_bytes=24 * MIB),
        name="combine",
    )(parts, ids, logits)


def body(
    queries,
    cached_key_rows,
    cached_value_rows,
    incoming_keys,
    incoming_values,
    lengths,
    residual,
    norm_gain,
    expert_ids,
    route_logits,
    w_gate,
    w_up,
    w_down,
):
    dev_count = lax.axis_size("dev")
    devices = lax.axis_size("grp") * dev_count
    group_rows = residual.shape[0]
    sent = attend(
        lengths, queries, cached_key_rows, cached_value_rows, incoming_keys, incoming_values,
        residual, devices,
    )
    rows = lax.all_to_all(sent, ("grp", "dev"), 0, 0, tiled=True)
    run_experts = experts if w_gate.shape[1] % 512 == 0 else experts_plain
    part = run_experts(rows, norm_gain, w_gate, w_up, w_down, group_rows, dev_count)
    got = lax.all_to_all(part, ("grp", "dev"), 0, 0, tiled=True)
    return combine(got, expert_ids, route_logits, dev_count)


def solution(mesh):
    return jax.shard_map(
        body,
        mesh=mesh,
        in_specs=(
            P(("grp", "dev"), None),
            P(("grp", "dev"), None, None),
            P(("grp", "dev"), None, None),
            P(("grp", "dev"), None),
            P(("grp", "dev"), None),
            P("grp"),
            P("grp", None),
            P(),
            P("grp", None),
            P("grp", None),
            P(None, ("dev", "grp")),
            P(None, ("dev", "grp")),
            P(("dev", "grp"), None),
        ),
        out_specs=P("grp", "dev"),
        check_vma=False,
    )
```

```python
import functools

import jax
import jax.numpy as jnp
from jax import lax
from jax.experimental import pallas as pl
from jax.experimental.pallas import tpu as pltpu
from jax.sharding import PartitionSpec as P

QUERY_HEADS = 48
KEY_VALUE_HEADS = 8
HEAD_SIZE = 128
E = 8
SHARING_DEVICES = 2
GROUP_WIDTH = QUERY_HEADS // KEY_VALUE_HEADS
LOCAL_HEADS = QUERY_HEADS // SHARING_DEVICES
MIB = 2**20
VMEM = pl.BlockSpec(memory_space=pltpu.VMEM)
HBM = pl.BlockSpec(memory_space=pltpu.HBM)
TILE = 512
EARLY_TILES = 0
HALF_TILE = 256
POOL = 9


def in_hbm(*arrays):
    return [pltpu.with_memory_space_constraint(a, pltpu.HBM) for a in arrays]


def in_vmem(*arrays):
    return [pltpu.with_memory_space_constraint(a, pltpu.VMEM) for a in arrays]


def head_rows(row):
    heads = row.shape[1] // HEAD_SIZE
    return jnp.concatenate(
        [row[:, j * HEAD_SIZE : (j + 1) * HEAD_SIZE] for j in range(heads)], axis=0
    )


def tile_source(w_gate, w_up, n):
    return (w_gate, w_up)[n % 2].at[:, pl.ds(n // 2 * TILE, TILE)]


def attend_kernel(early, *refs):
    lengths, queries, key_rows, value_rows, new_keys, new_values, residual = refs[:7]
    out = refs[7 + 2 * (early > 0)]
    buffers = refs[-9:-1]
    length_buf, query_buf, key_buf, value_buf, new_key_buf, new_value_buf, residual_buf = buffers[:7]
    sems, tile_sems = buffers[7], refs[-1]
    sequence, half = lax.axis_index("pair"), lax.axis_index("half")
    heads = LOCAL_HEADS
    columns = heads * HEAD_SIZE
    at = pl.ds(pl.multiple_of(half * columns, HEAD_SIZE), columns)
    pairs = [
        (key_rows.at[0], key_buf),
        (queries, query_buf),
        (new_keys, new_key_buf),
        (lengths, length_buf),
        (new_values, new_value_buf),
        (value_rows.at[0], value_buf),
        (residual.at[:, at], residual_buf),
    ]
    copies = [pltpu.make_async_copy(*pair, sems.at[i]) for i, pair in enumerate(pairs)]
    if early:
        w_gate, w_up, tiles = refs[7], refs[8], refs[10]
        tile_copies = [
            pltpu.make_async_copy(tile_source(w_gate, w_up, n), tiles.at[n], tile_sems.at[n])
            for n in range(early)
        ]
    else:
        tile_copies = []
    for copy in copies + tile_copies:
        copy.start()
    cache_len, width = key_buf.shape
    kv_heads = width // HEAD_SIZE
    scale = HEAD_SIZE ** (-0.5)
    for copy in copies[:4]:
        copy.wait()
    query = head_rows(query_buf[...].astype(jnp.float32))
    owner = lax.broadcasted_iota(jnp.int32, (heads, HEAD_SIZE), 0) // GROUP_WIDTH
    blocks = [jnp.where(owner == b, query, 0.0) for b in range(kv_heads)]
    spread = jnp.concatenate(blocks, axis=1)
    scores = (
        lax.dot_general(
            spread.astype(jnp.bfloat16),
            key_buf[...],
            (((1,), (1,)), ((), ())),
            preferred_element_type=jnp.float32,
        )
        * scale
    )
    places = lax.broadcasted_iota(jnp.int32, (heads, cache_len), 1)
    scores = jnp.where(places < length_buf[sequence], scores, -1e30)
    new_score = (
        jnp.sum(spread * new_key_buf[...].astype(jnp.float32), axis=1, keepdims=True) * scale
    )
    row_max = jnp.maximum(jnp.max(scores, axis=1, keepdims=True), new_score)
    exp_all = jnp.exp(scores - row_max)
    exp_new = jnp.exp(new_score - row_max)
    denom = jnp.sum(exp_all, axis=1, keepdims=True) + exp_new
    weights = (exp_all / denom).astype(jnp.bfloat16)
    weight_new = (exp_new / denom).astype(jnp.bfloat16).astype(jnp.float32)
    for copy in copies[4:]:
        copy.wait()
    mixed = jnp.dot(weights, value_buf[...], preferred_element_type=jnp.float32)
    mixed = mixed + weight_new * new_value_buf[...].astype(jnp.float32)
    attended = jnp.zeros((heads, HEAD_SIZE), jnp.float32)
    for b in range(kv_heads):
        attended = jnp.where(
            owner == b, mixed[:, b * HEAD_SIZE : (b + 1) * HEAD_SIZE], attended
        )
    attended = attended.astype(jnp.bfloat16).astype(jnp.float32)
    mine = residual_buf[...].astype(jnp.float32)
    rows = lax.broadcasted_iota(jnp.int32, mine.shape, 0)
    mine = jnp.sum(jnp.where(rows == sequence, mine, 0.0), axis=0, keepdims=True)
    out[...] = attended + head_rows(mine)
    for copy in tile_copies:
        copy.wait()


def attend(lengths, queries, key_rows, value_rows, new_keys, new_values, residual, w_gate, w_up, early):
    half_columns = LOCAL_HEADS * HEAD_SIZE
    out_shape = [jax.ShapeDtypeStruct((LOCAL_HEADS, HEAD_SIZE), jnp.float32)]
    operands = [lengths, queries, key_rows, value_rows, new_keys, new_values, residual]
    if early:
        out_shape.append(pltpu.VMEM((early, w_gate.shape[0], TILE), jnp.bfloat16))
        operands += [w_gate, w_up]
    return pl.pallas_call(
        functools.partial(attend_kernel, early),
        out_shape=out_shape,
        in_specs=[HBM] * len(operands),
        out_specs=[VMEM] * len(out_shape),
        scratch_shapes=[
            pltpu.SMEM(lengths.shape, jnp.int32),
            pltpu.VMEM(queries.shape, jnp.bfloat16),
            pltpu.VMEM(key_rows.shape[1:], jnp.bfloat16),
            pltpu.VMEM(value_rows.shape[1:], jnp.bfloat16),
            pltpu.VMEM(new_keys.shape, jnp.bfloat16),
            pltpu.VMEM(new_values.shape, jnp.bfloat16),
            pltpu.VMEM((residual.shape[0], half_columns), jnp.bfloat16),
            pltpu.SemaphoreType.DMA((7,)),
            pltpu.SemaphoreType.DMA((max(early, 1),)),
        ],
        compiler_params=pltpu.CompilerParams(vmem_limit_bytes=8 * MIB),
        name="attend",
    )(*in_hbm(*operands))


def norm_kernel(mine, other, gain, out):
    first = lax.axis_index("half") == 0
    row = jnp.concatenate(
        [jnp.where(first, mine[...], other[...]), jnp.where(first, other[...], mine[...])], axis=0
    )
    square = jnp.sum(jnp.sum(row * row, axis=0, keepdims=True), axis=1, keepdims=True)
    inverse = lax.rsqrt(square * (1.0 / (row.shape[0] * HEAD_SIZE)) + 1e-05)
    normed = (row * inverse * gain[...]).astype(jnp.bfloat16)
    out[...] = jnp.broadcast_to(normed[None], out.shape)


def norm(mine, other, gain, chips):
    heads = gain.shape[0] // HEAD_SIZE
    return pl.pallas_call(
        norm_kernel,
        out_shape=jax.ShapeDtypeStruct((chips, heads, HEAD_SIZE), jnp.bfloat16),
        in_specs=[VMEM] * 3,
        out_specs=VMEM,
        compiler_params=pltpu.CompilerParams(vmem_limit_bytes=16 * MIB),
        name="norm",
    )(mine, other, gain.reshape(heads, HEAD_SIZE))


def experts_kernel(
    parts, w_gate, w_up, w_down, out, flat, normed, hidden, pool, sems
):
    tokens, width = normed.shape
    local_hidden = w_down.shape[0]
    tiles = 2 * (local_hidden // TILE)
    held = []
    first = len(held)
    per_slot = width // local_hidden
    slots, heads = pool.shape[0], width // HEAD_SIZE
    group_rows, columns = out.shape[1:]
    targets = width // columns

    blocks = width // TILE
    items = [("tile", n) for n in range(first, tiles)]
    items += [("down", n) for n in range(0, blocks, per_slot)]

    def copies(i):
        kind, n = items[i]
        slot = i % slots
        if kind == "tile":
            return [pltpu.make_async_copy(tile_source(w_gate, w_up, n), pool.at[slot], sems.at[slot, 0])]
        return [
            pltpu.make_async_copy(
                w_down.at[:, pl.ds((n + k) * TILE, TILE)],
                pool.at[slot, pl.ds(k * local_hidden, local_hidden), :],
                sems.at[slot, k],
            )
            for k in range(per_slot)
        ]

    def begin(i):
        if i < len(items):
            for copy in copies(i):
                copy.start()

    for i in range(slots):
        begin(i)

    flat[...] = parts[...].astype(jnp.float32).reshape(flat.shape)
    for j in range(heads):
        normed[:, j * HEAD_SIZE : (j + 1) * HEAD_SIZE] = flat[
            pl.ds(j, tokens, stride=heads), :
        ].astype(jnp.bfloat16)

    for n in range(tiles):
        if n < first:
            weight = held[n][...]
        else:
            copies(n - first)[0].wait()
            weight = pool[(n - first) % slots]
        product = jnp.dot(normed[...], weight, preferred_element_type=jnp.float32)
        if n >= first:
            begin(n - first + slots)
        if n % 2 == 0:
            gate = product
        else:
            at = slice(n // 2 * TILE, (n // 2 + 1) * TILE)
            hidden[:, at] = (gate / (1.0 + jnp.exp(-gate)) * product).astype(jnp.bfloat16)

    step = HALF_TILE
    for i in range(tiles - first, len(items)):
        for k, copy in enumerate(copies(i)):
            copy.wait()
            weight = pool[i % slots, k * local_hidden : (k + 1) * local_hidden, :]
            part = jnp.dot(hidden[...], weight, preferred_element_type=jnp.float32)
            block = items[i][1] + k
            for q in range(TILE // step):
                target, column = divmod(block * TILE + q * step, columns)
                for g in range(tokens // group_rows):
                    out[g * targets + target, :, column : column + step] = part[
                        g * group_rows : (g + 1) * group_rows, q * step : (q + 1) * step
                    ].astype(out.dtype)
        begin(i + slots)


def experts(parts, w_gate, w_up, w_down, group_rows, dev_count):
    tokens = parts.shape[0]
    width, local_hidden = w_gate.shape
    columns = width // dev_count
    return pl.pallas_call(
        experts_kernel,
        out_shape=jax.ShapeDtypeStruct((SHARING_DEVICES * tokens, group_rows, columns), jnp.bfloat16),
        in_specs=[VMEM, HBM, HBM, HBM],
        out_specs=VMEM,
        scratch_shapes=[
            pltpu.VMEM((tokens * width // HEAD_SIZE, HEAD_SIZE), jnp.float32),
            pltpu.VMEM((tokens, width), jnp.bfloat16),
            pltpu.VMEM((tokens, local_hidden), jnp.bfloat16),
            pltpu.VMEM((POOL, width, TILE), jnp.bfloat16),
            pltpu.SemaphoreType.DMA((POOL, width // local_hidden)),
        ],
        compiler_params=pltpu.CompilerParams(vmem_limit_bytes=(6 * POOL + 2) * MIB),
        name="experts",
    )(*in_vmem(parts), *in_hbm(w_gate, w_up, w_down))


def experts_plain(parts, w_gate, w_up, w_down, group_rows, dev_count):
    width = w_gate.shape[0]
    normed = parts.reshape(-1, width)
    gate = jnp.dot(normed, w_gate, preferred_element_type=jnp.float32)
    up = jnp.dot(normed, w_up, preferred_element_type=jnp.float32)
    hidden = (jax.nn.silu(gate) * up).astype(jnp.bfloat16)
    part = jnp.dot(hidden, w_down, preferred_element_type=jnp.float32).astype(jnp.bfloat16)
    part = part.reshape(-1, group_rows, dev_count, width // dev_count)
    return part.transpose(0, 2, 1, 3).reshape(-1, group_rows, width // dev_count)


def combine_kernel(per_expert, dev_count, parts, ids, logits, out):
    shards = parts.shape[0] // dev_count
    logit = logits[...]
    top = jnp.max(logit, axis=1, keepdims=True)
    raised = jnp.exp(logit - top)
    probs = raised / jnp.sum(raised, axis=1, keepdims=True)
    chosen = ids[...]
    total = jnp.zeros(out.shape, jnp.float32)
    for e in range(E):
        weight = jnp.sum(jnp.where(chosen == e, probs, 0.0), axis=1, keepdims=True)
        here = jnp.zeros(out.shape, jnp.float32)
        for g in range(shards):
            for c in range(per_expert):
                here = here + parts[g * dev_count + e * per_expert + c].astype(jnp.float32)
        total = total + weight * here
    out[...] = total.astype(out.dtype)


def combine(parts, ids, logits, dev_count):
    return pl.pallas_call(
        functools.partial(combine_kernel, dev_count // E, dev_count),
        out_shape=jax.ShapeDtypeStruct(parts.shape[1:], jnp.bfloat16),
        in_specs=[VMEM] * 3,
        out_specs=VMEM,
        compiler_params=pltpu.CompilerParams(vmem_limit_bytes=24 * MIB),
        name="combine",
    )(parts, ids, logits)


def body(
    queries,
    cached_key_rows,
    cached_value_rows,
    incoming_keys,
    incoming_values,
    lengths,
    residual,
    norm_gain,
    expert_ids,
    route_logits,
    w_gate,
    w_up,
    w_down,
):
    chips = lax.axis_size("grp") * lax.axis_size("pair")
    dev_count = lax.axis_size("pair") * SHARING_DEVICES
    group_rows = residual.shape[0]
    streamed = w_gate.shape[1] == 4 * TILE
    summed, *early = attend(
        lengths, queries, cached_key_rows, cached_value_rows, incoming_keys, incoming_values,
        residual, w_gate, w_up, EARLY_TILES if streamed else 0,
    )
    other = lax.ppermute(summed, "half", [(0, 1), (1, 0)])
    sent = norm(summed, other, norm_gain, chips)
    rows = lax.all_to_all(sent, ("grp", "pair"), 0, 0, tiled=True)
    if streamed:
        part = experts(rows, *early, w_gate, w_up, w_down, group_rows, dev_count)
    else:
        part = experts_plain(rows, w_gate, w_up, w_down, group_rows, dev_count)
    got = lax.all_to_all(part, ("grp", "pair", "half"), 0, 0, tiled=True)
    return combine(got, expert_ids, route_logits, dev_count)


def solution(mesh):
    groups, dev_count = mesh.devices.shape
    split = jax.sharding.Mesh(
        mesh.devices.reshape(groups, dev_count // SHARING_DEVICES, SHARING_DEVICES),
        ("grp", "pair", "half"),
    )
    dev = ("pair", "half")
    rows = ("grp",) + dev
    shards = dev + ("grp",)
    return jax.shard_map(
        body,
        mesh=split,
        in_specs=(
            P(rows, None),
            P(rows, None, None),
            P(rows, None, None),
            P(rows, None),
            P(rows, None),
            P("grp"),
            P("grp", None),
            P(),
            P("grp", None),
            P("grp", None),
            P(None, shards),
            P(None, shards),
            P(shards, None),
        ),
        out_specs=P("grp", dev),
        check_vma=False,
    )
```

```python
import functools

import jax
import jax.numpy as jnp
from jax import lax
from jax.experimental import pallas as pl
from jax.experimental.pallas import tpu as pltpu
from jax.sharding import PartitionSpec as P

QUERY_HEADS = 48
KEY_VALUE_HEADS = 8
HEAD_SIZE = 128
E = 8
SHARING_DEVICES = 2
GROUP_WIDTH = QUERY_HEADS // KEY_VALUE_HEADS
LOCAL_HEADS = QUERY_HEADS // SHARING_DEVICES
MIB = 2**20
VMEM = pl.BlockSpec(memory_space=pltpu.VMEM)
HBM = pl.BlockSpec(memory_space=pltpu.HBM)
TILE = 512
PART = 256
RING = 6
UNTIL_ROWS = pl.CostEstimate(flops=40_000_000_000, bytes_accessed=0, transcendentals=0)


def in_hbm(*arrays):
    return [pltpu.with_memory_space_constraint(a, pltpu.HBM) for a in arrays]


def in_vmem(*arrays):
    return [pltpu.with_memory_space_constraint(a, pltpu.VMEM) for a in arrays]


def head_rows(row):
    heads = row.shape[1] // HEAD_SIZE
    return jnp.concatenate(
        [row[:, j * HEAD_SIZE : (j + 1) * HEAD_SIZE] for j in range(heads)], axis=0
    )


def attend_kernel(
    lengths, queries, key_rows, value_rows, new_keys, new_values, residual, out,
    length_buf, query_buf, key_buf, value_buf, new_key_buf, new_value_buf, residual_buf, sems,
):
    sequence, half = lax.axis_index("pair"), lax.axis_index("half")
    heads = LOCAL_HEADS
    columns = heads * HEAD_SIZE
    at = pl.ds(pl.multiple_of(half * columns, HEAD_SIZE), columns)
    pairs = [
        (key_rows.at[0], key_buf),
        (queries, query_buf),
        (new_keys, new_key_buf),
        (lengths, length_buf),
        (new_values, new_value_buf),
        (value_rows.at[0], value_buf),
        (residual.at[:, at], residual_buf),
    ]
    copies = [pltpu.make_async_copy(*pair, sems.at[i]) for i, pair in enumerate(pairs)]
    for copy in copies:
        copy.start()
    cache_len, width = key_buf.shape
    kv_heads = width // HEAD_SIZE
    scale = HEAD_SIZE ** (-0.5)
    for copy in copies[:4]:
        copy.wait()
    query = head_rows(query_buf[...].astype(jnp.float32))
    owner = lax.broadcasted_iota(jnp.int32, (heads, HEAD_SIZE), 0) // GROUP_WIDTH
    blocks = [jnp.where(owner == b, query, 0.0) for b in range(kv_heads)]
    spread = jnp.concatenate(blocks, axis=1)
    scores = (
        lax.dot_general(
            spread.astype(jnp.bfloat16),
            key_buf[...],
            (((1,), (1,)), ((), ())),
            preferred_element_type=jnp.float32,
        )
        * scale
    )
    places = lax.broadcasted_iota(jnp.int32, (heads, cache_len), 1)
    scores = jnp.where(places < length_buf[sequence], scores, -1e30)
    new_score = (
        jnp.sum(spread * new_key_buf[...].astype(jnp.float32), axis=1, keepdims=True) * scale
    )
    row_max = jnp.maximum(jnp.max(scores, axis=1, keepdims=True), new_score)
    exp_all = jnp.exp(scores - row_max)
    exp_new = jnp.exp(new_score - row_max)
    denom = jnp.sum(exp_all, axis=1, keepdims=True) + exp_new
    weights = (exp_all / denom).astype(jnp.bfloat16)
    weight_new = (exp_new / denom).astype(jnp.bfloat16).astype(jnp.float32)
    for copy in copies[4:]:
        copy.wait()
    mixed = jnp.dot(weights, value_buf[...], preferred_element_type=jnp.float32)
    mixed = mixed + weight_new * new_value_buf[...].astype(jnp.float32)
    attended = jnp.zeros((heads, HEAD_SIZE), jnp.float32)
    for b in range(kv_heads):
        attended = jnp.where(
            owner == b, mixed[:, b * HEAD_SIZE : (b + 1) * HEAD_SIZE], attended
        )
    attended = attended.astype(jnp.bfloat16).astype(jnp.float32)
    mine = residual_buf[...].astype(jnp.float32)
    rows = lax.broadcasted_iota(jnp.int32, mine.shape, 0)
    mine = jnp.sum(jnp.where(rows == sequence, mine, 0.0), axis=0, keepdims=True)
    out[...] = attended + head_rows(mine)


def attend(lengths, queries, key_rows, value_rows, new_keys, new_values, residual):
    half_columns = LOCAL_HEADS * HEAD_SIZE
    operands = [lengths, queries, key_rows, value_rows, new_keys, new_values, residual]
    return pl.pallas_call(
        attend_kernel,
        out_shape=jax.ShapeDtypeStruct((LOCAL_HEADS, HEAD_SIZE), jnp.float32),
        in_specs=[HBM] * len(operands),
        out_specs=VMEM,
        scratch_shapes=[
            pltpu.SMEM(lengths.shape, jnp.int32),
            pltpu.VMEM(queries.shape, jnp.bfloat16),
            pltpu.VMEM(key_rows.shape[1:], jnp.bfloat16),
            pltpu.VMEM(value_rows.shape[1:], jnp.bfloat16),
            pltpu.VMEM(new_keys.shape, jnp.bfloat16),
            pltpu.VMEM(new_values.shape, jnp.bfloat16),
            pltpu.VMEM((residual.shape[0], half_columns), jnp.bfloat16),
            pltpu.SemaphoreType.DMA((7,)),
        ],
        compiler_params=pltpu.CompilerParams(vmem_limit_bytes=4 * MIB),
        cost_estimate=UNTIL_ROWS,
        name="attend",
    )(*in_hbm(*operands))


def norm_kernel(mine, other, gain, out):
    first = lax.axis_index("half") == 0
    row = jnp.concatenate(
        [jnp.where(first, mine[...], other[...]), jnp.where(first, other[...], mine[...])], axis=0
    )
    square = jnp.sum(jnp.sum(row * row, axis=0, keepdims=True), axis=1, keepdims=True)
    inverse = lax.rsqrt(square * (1.0 / (row.shape[0] * HEAD_SIZE)) + 1e-05)
    normed = (row * inverse * gain[...]).astype(jnp.bfloat16)
    out[...] = jnp.broadcast_to(normed[None], out.shape)


def norm(mine, other, gain, chips):
    heads = gain.shape[0] // HEAD_SIZE
    return pl.pallas_call(
        norm_kernel,
        out_shape=jax.ShapeDtypeStruct((chips, heads, HEAD_SIZE), jnp.bfloat16),
        in_specs=[VMEM] * 3,
        out_specs=VMEM,
        compiler_params=pltpu.CompilerParams(vmem_limit_bytes=MIB + 4 * chips * gain.shape[0]),
        name="norm",
    )(mine, other, gain.reshape(heads, HEAD_SIZE))


def experts_kernel(parts, w_gate, w_up, w_down, out, flat, normed, hidden, ring, sems):
    tokens, width = normed.shape
    local_hidden = w_down.shape[0]
    slots, heads = ring.shape[0], width // HEAD_SIZE
    group_rows, columns = out.shape[1:]
    targets = width // columns
    blocks = width // TILE

    def down_copy(n):
        at = pl.ds(n * TILE, TILE)
        return pltpu.make_async_copy(w_down.at[:, at], ring.at[n % slots], sems.at[n % slots])

    for n in range(min(slots, blocks)):
        down_copy(n).start()

    flat[...] = parts[...].astype(jnp.float32).reshape(flat.shape)
    for j in range(heads):
        normed[:, j * HEAD_SIZE : (j + 1) * HEAD_SIZE] = flat[
            pl.ds(j, tokens, stride=heads), :
        ].astype(jnp.bfloat16)

    for n in range(local_hidden // TILE):
        at = slice(n * TILE, (n + 1) * TILE)
        gate = jnp.dot(normed[...], w_gate[:, at], preferred_element_type=jnp.float32)
        up = jnp.dot(normed[...], w_up[:, at], preferred_element_type=jnp.float32)
        hidden[:, at] = (gate / (1.0 + jnp.exp(-gate)) * up).astype(jnp.bfloat16)

    for n in range(blocks):
        down_copy(n).wait()
        part = jnp.dot(hidden[...], ring[n % slots], preferred_element_type=jnp.float32)
        if n + slots < blocks:
            down_copy(n + slots).start()
        for q in range(0, TILE, PART):
            target, column = divmod(n * TILE + q, columns)
            for g in range(tokens // group_rows):
                out[g * targets + target, :, column : column + PART] = part[
                    g * group_rows : (g + 1) * group_rows, q : q + PART
                ].astype(out.dtype)


def experts(parts, w_gate, w_up, w_down, group_rows, dev_count):
    tokens = parts.shape[0]
    width, local_hidden = w_gate.shape
    columns = width // dev_count
    return pl.pallas_call(
        experts_kernel,
        out_shape=jax.ShapeDtypeStruct((SHARING_DEVICES * tokens, group_rows, columns), jnp.bfloat16),
        in_specs=[VMEM, VMEM, VMEM, HBM],
        out_specs=VMEM,
        scratch_shapes=[
            pltpu.VMEM((tokens * width // HEAD_SIZE, HEAD_SIZE), jnp.float32),
            pltpu.VMEM((tokens, width), jnp.bfloat16),
            pltpu.VMEM((tokens, local_hidden), jnp.bfloat16),
            pltpu.VMEM((RING, local_hidden, TILE), jnp.bfloat16),
            pltpu.SemaphoreType.DMA((RING,)),
        ],
        compiler_params=pltpu.CompilerParams(vmem_limit_bytes=(2 * RING + 1) * MIB),
        name="experts",
    )(*in_vmem(parts, w_gate, w_up), *in_hbm(w_down))


def experts_plain(parts, w_gate, w_up, w_down, group_rows, dev_count):
    width = w_gate.shape[0]
    normed = parts.reshape(-1, width)
    gate = jnp.dot(normed, w_gate, preferred_element_type=jnp.float32)
    up = jnp.dot(normed, w_up, preferred_element_type=jnp.float32)
    hidden = (jax.nn.silu(gate) * up).astype(jnp.bfloat16)
    part = jnp.dot(hidden, w_down, preferred_element_type=jnp.float32).astype(jnp.bfloat16)
    part = part.reshape(-1, group_rows, dev_count, width // dev_count)
    return part.transpose(0, 2, 1, 3).reshape(-1, group_rows, width // dev_count)


def combine_kernel(per_expert, dev_count, parts, ids, logits, out):
    shards = parts.shape[0] // dev_count
    logit = logits[...]
    top = jnp.max(logit, axis=1, keepdims=True)
    raised = jnp.exp(logit - top)
    probs = raised / jnp.sum(raised, axis=1, keepdims=True)
    chosen = ids[...]
    total = jnp.zeros(out.shape, jnp.float32)
    for e in range(E):
        weight = jnp.sum(jnp.where(chosen == e, probs, 0.0), axis=1, keepdims=True)
        here = jnp.zeros(out.shape, jnp.float32)
        for g in range(shards):
            for c in range(per_expert):
                here = here + parts[g * dev_count + e * per_expert + c].astype(jnp.float32)
        total = total + weight * here
    out[...] = total.astype(out.dtype)


def combine(parts, ids, logits, dev_count):
    return pl.pallas_call(
        functools.partial(combine_kernel, dev_count // E, dev_count),
        out_shape=jax.ShapeDtypeStruct(parts.shape[1:], jnp.bfloat16),
        in_specs=[VMEM] * 3,
        out_specs=VMEM,
        compiler_params=pltpu.CompilerParams(vmem_limit_bytes=24 * MIB),
        name="combine",
    )(parts, ids, logits)


def body(
    queries,
    cached_key_rows,
    cached_value_rows,
    incoming_keys,
    incoming_values,
    lengths,
    residual,
    norm_gain,
    expert_ids,
    route_logits,
    w_gate,
    w_up,
    w_down,
):
    chips = lax.axis_size("grp") * lax.axis_size("pair")
    dev_count = lax.axis_size("pair") * SHARING_DEVICES
    group_rows = residual.shape[0]
    summed = attend(
        lengths, queries, cached_key_rows, cached_value_rows, incoming_keys, incoming_values, residual
    )
    other = lax.ppermute(summed, "half", [(0, 1), (1, 0)])
    sent = norm(summed, other, norm_gain, chips)
    rows = lax.all_to_all(sent, ("grp", "pair"), 0, 0, tiled=True)
    whole_blocks = w_gate.shape[1] % TILE == 0 and norm_gain.shape[0] // dev_count % PART == 0
    run_experts = experts if whole_blocks else experts_plain
    part = run_experts(rows, w_gate, w_up, w_down, group_rows, dev_count)
    got = lax.all_to_all(part, ("grp", "pair", "half"), 0, 0, tiled=True)
    return combine(got, expert_ids, route_logits, dev_count)


def solution(mesh):
    groups, dev_count = mesh.devices.shape
    split = jax.sharding.Mesh(
        mesh.devices.reshape(groups, dev_count // SHARING_DEVICES, SHARING_DEVICES),
        ("grp", "pair", "half"),
    )
    dev = ("pair", "half")
    rows = ("grp",) + dev
    shards = dev + ("grp",)
    return jax.shard_map(
        body,
        mesh=split,
        in_specs=(
            P(rows, None),
            P(rows, None, None),
            P(rows, None, None),
            P(rows, None),
            P(rows, None),
            P("grp"),
            P("grp", None),
            P(),
            P("grp", None),
            P("grp", None),
            P(None, shards),
            P(None, shards),
            P(shards, None),
        ),
        out_specs=P("grp", dev),
        check_vma=False,
    )
```

```python
import functools

import jax
import jax.numpy as jnp
from jax import lax
from jax.experimental import pallas as pl
from jax.experimental.pallas import tpu as pltpu
from jax.sharding import PartitionSpec as P

QUERY_HEADS = 48
KEY_VALUE_HEADS = 8
HEAD_SIZE = 128
E = 8
SHARING_DEVICES = 2
GROUP_WIDTH = QUERY_HEADS // KEY_VALUE_HEADS
LOCAL_HEADS = QUERY_HEADS // SHARING_DEVICES
MIB = 2**20
VMEM = pl.BlockSpec(memory_space=pltpu.VMEM)
HBM = pl.BlockSpec(memory_space=pltpu.HBM)
TILE = 512
PART = 256
RING = 6
PASSES = 2
DOWN = 1024
UNTIL_ROWS = pl.CostEstimate(flops=40_000_000_000, bytes_accessed=0, transcendentals=0)


def in_hbm(*arrays):
    return [pltpu.with_memory_space_constraint(a, pltpu.HBM) for a in arrays]


def in_vmem(*arrays):
    return [pltpu.with_memory_space_constraint(a, pltpu.VMEM) for a in arrays]


def head_rows(row):
    heads = row.shape[1] // HEAD_SIZE
    return jnp.concatenate(
        [row[:, j * HEAD_SIZE : (j + 1) * HEAD_SIZE] for j in range(heads)], axis=0
    )


def as_column(row, diagonal):
    return jnp.sum(jnp.where(diagonal, row, jnp.zeros_like(row)), axis=1, keepdims=True)


def attend_kernel(
    lengths, queries, key_rows, value_rows, new_keys, new_values, residual, ids, logits, out, weights_out,
    length_buf, query_buf, key_buf, value_buf, new_key_buf, new_value_buf, residual_buf, id_buf, logit_buf,
    sems,
):
    sequence, half = lax.axis_index("pair"), lax.axis_index("half")
    heads = LOCAL_HEADS
    columns = heads * HEAD_SIZE
    at = pl.ds(pl.multiple_of(half * columns, HEAD_SIZE), columns)
    pairs = [
        (key_rows.at[0], key_buf),
        (queries, query_buf),
        (new_keys, new_key_buf),
        (lengths, length_buf),
        (new_values, new_value_buf),
        (value_rows.at[0], value_buf),
        (residual.at[:, at], residual_buf),
        (ids, id_buf),
        (logits, logit_buf),
    ]
    copies = [pltpu.make_async_copy(*pair, sems.at[i]) for i, pair in enumerate(pairs)]
    for copy in copies:
        copy.start()
    cache_len, width = key_buf.shape
    kv_heads = width // HEAD_SIZE
    scale = HEAD_SIZE ** (-0.5)
    for copy in copies[:4]:
        copy.wait()
    query = head_rows(query_buf[...].astype(jnp.float32))
    owner = lax.broadcasted_iota(jnp.int32, (heads, HEAD_SIZE), 0) // GROUP_WIDTH
    blocks = [jnp.where(owner == b, query, 0.0) for b in range(kv_heads)]
    spread = jnp.concatenate(blocks, axis=1)
    scores = (
        lax.dot_general(
            spread.astype(jnp.bfloat16),
            key_buf[...],
            (((1,), (1,)), ((), ())),
            preferred_element_type=jnp.float32,
        )
        * scale
    )
    places = lax.broadcasted_iota(jnp.int32, (heads, cache_len), 1)
    scores = jnp.where(places < length_buf[sequence], scores, -1e30)
    new_score = (
        jnp.sum(spread * new_key_buf[...].astype(jnp.float32), axis=1, keepdims=True) * scale
    )
    row_max = jnp.maximum(jnp.max(scores, axis=1, keepdims=True), new_score)
    exp_all = jnp.exp(scores - row_max)
    exp_new = jnp.exp(new_score - row_max)
    denom = jnp.sum(exp_all, axis=1, keepdims=True) + exp_new
    weights = (exp_all / denom).astype(jnp.bfloat16)
    weight_new = (exp_new / denom).astype(jnp.bfloat16).astype(jnp.float32)
    for copy in copies[4:]:
        copy.wait()
    mixed = jnp.dot(weights, value_buf[...], preferred_element_type=jnp.float32)
    mixed = mixed + weight_new * new_value_buf[...].astype(jnp.float32)
    attended = jnp.zeros((heads, HEAD_SIZE), jnp.float32)
    for b in range(kv_heads):
        attended = jnp.where(
            owner == b, mixed[:, b * HEAD_SIZE : (b + 1) * HEAD_SIZE], attended
        )
    attended = attended.astype(jnp.bfloat16).astype(jnp.float32)
    mine = residual_buf[...].astype(jnp.float32)
    rows = lax.broadcasted_iota(jnp.int32, mine.shape, 0)
    mine = jnp.sum(jnp.where(rows == sequence, mine, 0.0), axis=0, keepdims=True)
    out[...] = attended + head_rows(mine)

    count, tokens = id_buf.shape
    diagonal = lax.broadcasted_iota(jnp.int32, (tokens, tokens), 0) == lax.broadcasted_iota(
        jnp.int32, (tokens, tokens), 1
    )
    chosen = [as_column(id_buf[k : k + 1, :], diagonal) for k in range(count)]
    logit = [as_column(logit_buf[k : k + 1, :], diagonal) for k in range(count)]
    top = functools.reduce(jnp.maximum, logit)
    raised = [jnp.exp(v - top) for v in logit]
    scale = 1.0 / functools.reduce(jnp.add, raised)
    expert = lax.broadcasted_iota(jnp.int32, weights_out.shape, 1)
    by_expert = jnp.zeros(weights_out.shape, jnp.float32)
    for k in range(count):
        by_expert = by_expert + jnp.where(chosen[k] == expert, raised[k] * scale, 0.0)
    weights_out[...] = by_expert


def attend(lengths, queries, key_rows, value_rows, new_keys, new_values, residual, ids, logits):
    half_columns = LOCAL_HEADS * HEAD_SIZE
    operands = [lengths, queries, key_rows, value_rows, new_keys, new_values, residual, ids.T, logits.T]
    return pl.pallas_call(
        attend_kernel,
        out_shape=(
            jax.ShapeDtypeStruct((LOCAL_HEADS, HEAD_SIZE), jnp.float32),
            jax.ShapeDtypeStruct((ids.shape[0], E), jnp.float32),
        ),
        in_specs=[HBM] * len(operands),
        out_specs=(VMEM, VMEM),
        scratch_shapes=[
            pltpu.SMEM(lengths.shape, jnp.int32),
            pltpu.VMEM(queries.shape, jnp.bfloat16),
            pltpu.VMEM(key_rows.shape[1:], jnp.bfloat16),
            pltpu.VMEM(value_rows.shape[1:], jnp.bfloat16),
            pltpu.VMEM(new_keys.shape, jnp.bfloat16),
            pltpu.VMEM(new_values.shape, jnp.bfloat16),
            pltpu.VMEM((residual.shape[0], half_columns), jnp.bfloat16),
            pltpu.VMEM(ids.shape[::-1], jnp.int32),
            pltpu.VMEM(logits.shape[::-1], jnp.float32),
            pltpu.SemaphoreType.DMA((len(operands),)),
        ],
        compiler_params=pltpu.CompilerParams(vmem_limit_bytes=4 * MIB),
        cost_estimate=UNTIL_ROWS,
        name="attend",
    )(*in_hbm(*operands))


def norm_kernel(mine, other, gain, out):
    first = lax.axis_index("half") == 0
    row = jnp.concatenate(
        [jnp.where(first, mine[...], other[...]), jnp.where(first, other[...], mine[...])], axis=0
    )
    square = jnp.sum(jnp.sum(row * row, axis=0, keepdims=True), axis=1, keepdims=True)
    inverse = lax.rsqrt(square * (1.0 / (row.shape[0] * HEAD_SIZE)) + 1e-05)
    normed = (row * inverse * gain[...]).astype(jnp.bfloat16)
    out[...] = jnp.broadcast_to(normed[None], out.shape)


def norm(mine, other, gain, chips):
    heads = gain.shape[0] // HEAD_SIZE
    return pl.pallas_call(
        norm_kernel,
        out_shape=jax.ShapeDtypeStruct((chips, heads, HEAD_SIZE), jnp.bfloat16),
        in_specs=[VMEM] * 3,
        out_specs=VMEM,
        compiler_params=pltpu.CompilerParams(vmem_limit_bytes=MIB + 4 * chips * gain.shape[0]),
        name="norm",
    )(mine, other, gain.reshape(heads, HEAD_SIZE))


def experts_kernel(
    parts, w_gate, w_up, w_down, out, flat, normed, hidden, total, ring, sems
):
    tokens, width = normed.shape
    local_hidden = hidden.shape[1]
    slots, units = ring.shape[:2]
    heads = width // HEAD_SIZE
    group_rows, columns = out.shape[1:]
    targets = width // columns
    blocks = width // DOWN

    def down_copy(i):
        which, n = divmod(i, blocks)
        source = w_down.at[pl.ds(which * units, units), pl.ds(n * DOWN, DOWN)]
        return pltpu.make_async_copy(source, ring.at[i % slots], sems.at[i % slots])

    for i in range(min(slots, PASSES * blocks)):
        down_copy(i).start()

    flat[...] = parts[...].astype(jnp.float32).reshape(flat.shape)
    for j in range(heads):
        normed[:, j * HEAD_SIZE : (j + 1) * HEAD_SIZE] = flat[
            pl.ds(j, tokens, stride=heads), :
        ].astype(jnp.bfloat16)

    for which in range(PASSES):
        mine = slice(which * units, (which + 1) * units)
        for start in range(which * units, (which + 1) * units, TILE):
            at = slice(start, start + TILE)
            gate = jnp.dot(normed[...], w_gate[:, at], preferred_element_type=jnp.float32)
            up = jnp.dot(normed[...], w_up[:, at], preferred_element_type=jnp.float32)
            hidden[:, at] = (gate / (1.0 + jnp.exp(-gate)) * up).astype(jnp.bfloat16)
        for n in range(blocks):
            i = which * blocks + n
            down_copy(i).wait()
            part = jnp.dot(hidden[:, mine], ring[i % slots], preferred_element_type=jnp.float32)
            if i + slots < PASSES * blocks:
                down_copy(i + slots).start()
            at = slice(n * DOWN, (n + 1) * DOWN)
            if which > 0:
                part = total[:, at] + part
            if which < PASSES - 1:
                total[:, at] = part
                continue
            for q in range(0, DOWN, PART):
                target, column = divmod(n * DOWN + q, columns)
                for g in range(tokens // group_rows):
                    out[g * targets + target, :, column : column + PART] = part[
                        g * group_rows : (g + 1) * group_rows, q : q + PART
                    ].astype(out.dtype)


def experts(parts, w_gate, w_up, w_down, group_rows, dev_count):
    tokens = parts.shape[0]
    width, local_hidden = w_gate.shape
    columns = width // dev_count
    units = local_hidden // PASSES
    return pl.pallas_call(
        experts_kernel,
        out_shape=jax.ShapeDtypeStruct((SHARING_DEVICES * tokens, group_rows, columns), jnp.bfloat16),
        in_specs=[VMEM, VMEM, VMEM, HBM],
        out_specs=VMEM,
        scratch_shapes=[
            pltpu.VMEM((tokens * width // HEAD_SIZE, HEAD_SIZE), jnp.float32),
            pltpu.VMEM((tokens, width), jnp.bfloat16),
            pltpu.VMEM((tokens, local_hidden), jnp.bfloat16),
            pltpu.VMEM((tokens, width), jnp.float32),
            pltpu.VMEM((RING, units, DOWN), jnp.bfloat16),
            pltpu.SemaphoreType.DMA((RING,)),
        ],
        compiler_params=pltpu.CompilerParams(vmem_limit_bytes=RING * units * DOWN * 2 + 2 * MIB),
        name="experts",
    )(*in_vmem(parts, w_gate, w_up), *in_hbm(w_down))


def experts_plain(parts, w_gate, w_up, w_down, group_rows, dev_count):
    width = w_gate.shape[0]
    normed = parts.reshape(-1, width)
    gate = jnp.dot(normed, w_gate, preferred_element_type=jnp.float32)
    up = jnp.dot(normed, w_up, preferred_element_type=jnp.float32)
    hidden = (jax.nn.silu(gate) * up).astype(jnp.bfloat16)
    part = jnp.dot(hidden, w_down, preferred_element_type=jnp.float32).astype(jnp.bfloat16)
    part = part.reshape(-1, group_rows, dev_count, width // dev_count)
    return part.transpose(0, 2, 1, 3).reshape(-1, group_rows, width // dev_count)


def combine_kernel(per_expert, dev_count, parts, weights, out):
    shards = parts.shape[0] // dev_count
    weight = weights[...]
    total = jnp.zeros(out.shape, jnp.float32)
    for e in range(E):
        here = jnp.zeros(out.shape, jnp.float32)
        for g in range(shards):
            for c in range(per_expert):
                here = here + parts[g * dev_count + e * per_expert + c].astype(jnp.float32)
        total = total + weight[:, e : e + 1] * here
    out[...] = total.astype(out.dtype)


def combine(parts, weights, dev_count):
    return pl.pallas_call(
        functools.partial(combine_kernel, dev_count // E, dev_count),
        out_shape=jax.ShapeDtypeStruct(parts.shape[1:], jnp.bfloat16),
        in_specs=[VMEM] * 2,
        out_specs=VMEM,
        compiler_params=pltpu.CompilerParams(vmem_limit_bytes=24 * MIB),
        name="combine",
    )(*in_vmem(parts, weights))


def body(
    queries,
    cached_key_rows,
    cached_value_rows,
    incoming_keys,
    incoming_values,
    lengths,
    residual,
    norm_gain,
    expert_ids,
    route_logits,
    w_gate,
    w_up,
    w_down,
):
    chips = lax.axis_size("grp") * lax.axis_size("pair")
    dev_count = lax.axis_size("pair") * SHARING_DEVICES
    group_rows = residual.shape[0]
    summed, weights = attend(
        lengths, queries, cached_key_rows, cached_value_rows, incoming_keys, incoming_values,
        residual, expert_ids, route_logits,
    )
    other = lax.ppermute(summed, "half", [(0, 1), (1, 0)])
    sent = norm(summed, other, norm_gain, chips)
    rows = lax.all_to_all(sent, ("grp", "pair"), 0, 0, tiled=True)
    whole_blocks = w_gate.shape[1] % (PASSES * TILE) == 0 and norm_gain.shape[0] // dev_count % PART == 0
    run_experts = experts if whole_blocks else experts_plain
    part = run_experts(rows, w_gate, w_up, w_down, group_rows, dev_count)
    got = lax.all_to_all(part, ("grp", "pair", "half"), 0, 0, tiled=True)
    return combine(got, weights, dev_count)


def solution(mesh):
    groups, dev_count = mesh.devices.shape
    split = jax.sharding.Mesh(
        mesh.devices.reshape(groups, dev_count // SHARING_DEVICES, SHARING_DEVICES),
        ("grp", "pair", "half"),
    )
    dev = ("pair", "half")
    rows = ("grp",) + dev
    shards = dev + ("grp",)
    return jax.shard_map(
        body,
        mesh=split,
        in_specs=(
            P(rows, None),
            P(rows, None, None),
            P(rows, None, None),
            P(rows, None),
            P(rows, None),
            P("grp"),
            P("grp", None),
            P(),
            P("grp", None),
            P("grp", None),
            P(None, shards),
            P(None, shards),
            P(shards, None),
        ),
        out_specs=P("grp", dev),
        check_vma=False,
    )
```

```python
import functools

import jax
import jax.numpy as jnp
from jax import lax
from jax.experimental import pallas as pl
from jax.experimental.pallas import tpu as pltpu
from jax.sharding import PartitionSpec as P

QUERY_HEADS = 48
KEY_VALUE_HEADS = 8
HEAD_SIZE = 128
E = 8
SHARING_DEVICES = 2
GROUP_WIDTH = QUERY_HEADS // KEY_VALUE_HEADS
LOCAL_HEADS = QUERY_HEADS // SHARING_DEVICES
MIB = 2**20
VMEM = pl.BlockSpec(memory_space=pltpu.VMEM)
HBM = pl.BlockSpec(memory_space=pltpu.HBM)
MXU = 256
TILE = 512
PART = 256
RING = 6
PASSES = 2
DOWN = 1024
UNTIL_ROWS = pl.CostEstimate(flops=40_000_000_000, bytes_accessed=0, transcendentals=0)


def in_hbm(*arrays):
    return [pltpu.with_memory_space_constraint(a, pltpu.HBM) for a in arrays]


def in_vmem(*arrays):
    return [pltpu.with_memory_space_constraint(a, pltpu.VMEM) for a in arrays]


def head_rows(row):
    heads = row.shape[1] // HEAD_SIZE
    return jnp.concatenate(
        [row[:, j * HEAD_SIZE : (j + 1) * HEAD_SIZE] for j in range(heads)], axis=0
    )


def as_column(row, diagonal):
    return jnp.sum(jnp.where(diagonal, row, jnp.zeros_like(row)), axis=1, keepdims=True)


def attend_kernel(
    lengths, queries, key_rows, value_rows, new_keys, new_values, residual, ids, logits, out, weights_out,
    length_buf, query_buf, key_buf, value_buf, new_key_buf, new_value_buf, residual_buf, id_buf, logit_buf,
    sems,
):
    sequence, half = lax.axis_index("pair"), lax.axis_index("half")
    heads = LOCAL_HEADS
    columns = heads * HEAD_SIZE
    at = pl.ds(pl.multiple_of(half * columns, HEAD_SIZE), columns)
    pairs = [
        (key_rows.at[0], key_buf),
        (queries, query_buf),
        (new_keys, new_key_buf),
        (lengths, length_buf),
        (new_values, new_value_buf),
        (value_rows.at[0], value_buf),
        (residual.at[:, at], residual_buf),
        (ids, id_buf),
        (logits, logit_buf),
    ]
    copies = [pltpu.make_async_copy(*pair, sems.at[i]) for i, pair in enumerate(pairs)]
    for copy in copies:
        copy.start()
    cache_len, width = key_buf.shape
    kv_heads = width // HEAD_SIZE
    scale = HEAD_SIZE ** (-0.5)
    for copy in copies[:4]:
        copy.wait()
    query = head_rows(query_buf[...].astype(jnp.float32))
    owner = lax.broadcasted_iota(jnp.int32, (heads, HEAD_SIZE), 0) // GROUP_WIDTH
    blocks = [jnp.where(owner == b, query, 0.0) for b in range(kv_heads)]
    spread = jnp.concatenate(blocks, axis=1)
    scores = (
        lax.dot_general(
            spread.astype(jnp.bfloat16),
            key_buf[...],
            (((1,), (1,)), ((), ())),
            preferred_element_type=jnp.float32,
        )
        * scale
    )
    places = lax.broadcasted_iota(jnp.int32, (heads, cache_len), 1)
    scores = jnp.where(places < length_buf[sequence], scores, -1e30)
    new_score = (
        jnp.sum(spread * new_key_buf[...].astype(jnp.float32), axis=1, keepdims=True) * scale
    )
    row_max = jnp.maximum(jnp.max(scores, axis=1, keepdims=True), new_score)
    exp_all = jnp.exp(scores - row_max)
    exp_new = jnp.exp(new_score - row_max)
    denom = jnp.sum(exp_all, axis=1, keepdims=True) + exp_new
    weights = (exp_all / denom).astype(jnp.bfloat16)
    weight_new = (exp_new / denom).astype(jnp.bfloat16).astype(jnp.float32)
    for copy in copies[4:]:
        copy.wait()
    mixed = jnp.dot(weights, value_buf[...], preferred_element_type=jnp.float32)
    mixed = mixed + weight_new * new_value_buf[...].astype(jnp.float32)
    attended = jnp.zeros((heads, HEAD_SIZE), jnp.float32)
    for b in range(kv_heads):
        attended = jnp.where(
            owner == b, mixed[:, b * HEAD_SIZE : (b + 1) * HEAD_SIZE], attended
        )
    attended = attended.astype(jnp.bfloat16).astype(jnp.float32)
    mine = residual_buf[...].astype(jnp.float32)
    rows = lax.broadcasted_iota(jnp.int32, mine.shape, 0)
    mine = jnp.sum(jnp.where(rows == sequence, mine, 0.0), axis=0, keepdims=True)
    out[...] = attended + head_rows(mine)

    count, tokens = id_buf.shape
    diagonal = lax.broadcasted_iota(jnp.int32, (tokens, tokens), 0) == lax.broadcasted_iota(
        jnp.int32, (tokens, tokens), 1
    )
    chosen = [as_column(id_buf[k : k + 1, :], diagonal) for k in range(count)]
    logit = [as_column(logit_buf[k : k + 1, :], diagonal) for k in range(count)]
    top = functools.reduce(jnp.maximum, logit)
    raised = [jnp.exp(v - top) for v in logit]
    scale = 1.0 / functools.reduce(jnp.add, raised)
    expert = lax.broadcasted_iota(jnp.int32, weights_out.shape, 1)
    by_expert = jnp.zeros(weights_out.shape, jnp.float32)
    for k in range(count):
        by_expert = by_expert + jnp.where(chosen[k] == expert, raised[k] * scale, 0.0)
    weights_out[...] = by_expert


def attend(lengths, queries, key_rows, value_rows, new_keys, new_values, residual, ids, logits):
    half_columns = LOCAL_HEADS * HEAD_SIZE
    operands = [lengths, queries, key_rows, value_rows, new_keys, new_values, residual, ids.T, logits.T]
    return pl.pallas_call(
        attend_kernel,
        out_shape=(
            jax.ShapeDtypeStruct((LOCAL_HEADS, HEAD_SIZE), jnp.float32),
            jax.ShapeDtypeStruct((ids.shape[0], E), jnp.float32),
        ),
        in_specs=[HBM] * len(operands),
        out_specs=(VMEM, VMEM),
        scratch_shapes=[
            pltpu.SMEM(lengths.shape, jnp.int32),
            pltpu.VMEM(queries.shape, jnp.bfloat16),
            pltpu.VMEM(key_rows.shape[1:], jnp.bfloat16),
            pltpu.VMEM(value_rows.shape[1:], jnp.bfloat16),
            pltpu.VMEM(new_keys.shape, jnp.bfloat16),
            pltpu.VMEM(new_values.shape, jnp.bfloat16),
            pltpu.VMEM((residual.shape[0], half_columns), jnp.bfloat16),
            pltpu.VMEM(ids.shape[::-1], jnp.int32),
            pltpu.VMEM(logits.shape[::-1], jnp.float32),
            pltpu.SemaphoreType.DMA((len(operands),)),
        ],
        compiler_params=pltpu.CompilerParams(vmem_limit_bytes=4 * MIB),
        cost_estimate=UNTIL_ROWS,
        name="attend",
    )(*in_hbm(*operands))


def norm_kernel(mine, other, gain, out):
    first = lax.axis_index("half") == 0
    row = jnp.concatenate(
        [jnp.where(first, mine[...], other[...]), jnp.where(first, other[...], mine[...])], axis=0
    )
    square = jnp.sum(jnp.sum(row * row, axis=0, keepdims=True), axis=1, keepdims=True)
    inverse = lax.rsqrt(square * (1.0 / (row.shape[0] * HEAD_SIZE)) + 1e-05)
    normed = (row * inverse * gain[...]).astype(jnp.bfloat16)
    out[...] = jnp.broadcast_to(normed[None], out.shape)


def norm(mine, other, gain, chips):
    heads = gain.shape[0] // HEAD_SIZE
    return pl.pallas_call(
        norm_kernel,
        out_shape=jax.ShapeDtypeStruct((chips, heads, HEAD_SIZE), jnp.bfloat16),
        in_specs=[VMEM] * 3,
        out_specs=VMEM,
        compiler_params=pltpu.CompilerParams(vmem_limit_bytes=MIB + 4 * chips * gain.shape[0]),
        name="norm",
    )(mine, other, gain.reshape(heads, HEAD_SIZE))


class Job:
    def __init__(self, rows, weight, before, after, after_rows):
        self.rows, self.weight, self.before, self.after = rows, weight, before, after
        self.after_rows = after_rows


def run_jobs(jobs, sums):
    steps = [(n, k) for n, job in enumerate(jobs) for k in range(0, job.rows.shape[1], MXU)]

    def push(i):
        n, k = steps[i]
        job = jobs[n]
        if k == 0:
            job.before()
        for m in range(2):
            tile = job.weight[k : k + MXU, m * MXU : (m + 1) * MXU]
            pltpu.matmul_push_rhs(tile, i % 2, m)

    pending = []

    def settle():
        while pending:
            n = pending.pop()
            jobs[n].after([pltpu.matmul_pop(sums[n % 2][m]) for m in range(2)])

    push(0)
    for i, (n, k) in enumerate(steps):
        if i + 1 < len(steps):
            push(i + 1)
        job = jobs[n]
        if k == 0 and job.after_rows:
            settle()
        for m in range(2):
            pltpu.matmul_acc_lhs(sums[n % 2][m], job.rows[:, k : k + MXU], load_staged_rhs=i % 2)
        settle()
        if k + MXU == job.rows.shape[1]:
            pending.append(n)
    settle()


def experts_kernel(
    parts, w_gate, w_up, w_down, out, flat, normed, hidden, gates, total, ring, sems
):
    tokens, width = normed.shape
    slots, units = ring.shape[:2]
    heads = width // HEAD_SIZE
    group_rows, columns = out.shape[1:]
    targets = width // columns
    blocks = width // DOWN

    def down_copy(i):
        which, n = divmod(i, blocks)
        source = w_down.at[pl.ds(which * units, units), pl.ds(n * DOWN, DOWN)]
        return pltpu.make_async_copy(source, ring.at[i % slots], sems.at[i % slots])

    for i in range(min(slots, PASSES * blocks)):
        down_copy(i).start()

    flat[...] = parts[...].astype(jnp.float32).reshape(flat.shape)
    for j in range(heads):
        normed[:, j * HEAD_SIZE : (j + 1) * HEAD_SIZE] = flat[
            pl.ds(j, tokens, stride=heads), :
        ].astype(jnp.bfloat16)

    def nothing():
        pass

    def gate_done(start):
        def after(sums):
            for m in range(2):
                gates[:, m * MXU : (m + 1) * MXU] = sums[m]

        return after

    def up_done(start):
        def after(sums):
            for m in range(2):
                gate = gates[:, m * MXU : (m + 1) * MXU]
                at = slice(start + m * MXU, start + (m + 1) * MXU)
                hidden[:, at] = (gate / (1.0 + jnp.exp(-gate)) * sums[m]).astype(jnp.bfloat16)

        return after

    def down_done(which, i, start):
        def after(sums):
            for m in range(2):
                column = start + m * MXU
                part = sums[m]
                at = slice(column, column + MXU)
                if which > 0:
                    part = total[:, at] + part
                if which < PASSES - 1:
                    total[:, at] = part
                    continue
                target, place = divmod(column, columns)
                for g in range(tokens // group_rows):
                    out[g * targets + target, :, place : place + MXU] = part[
                        g * group_rows : (g + 1) * group_rows
                    ].astype(out.dtype)
            if (start + 2 * MXU) % DOWN == 0 and i + slots < PASSES * blocks:
                down_copy(i + slots).start()

        return after

    jobs = []
    for which in range(PASSES):
        for start in range(which * units, (which + 1) * units, 2 * MXU):
            at = pl.ds(start, 2 * MXU)
            jobs.append(Job(normed, w_gate.at[:, at], nothing, gate_done(start), False))
            jobs.append(Job(normed, w_up.at[:, at], nothing, up_done(start), False))
        mine = hidden.at[:, pl.ds(which * units, units)]
        for n in range(blocks):
            i = which * blocks + n
            for start in range(0, DOWN, 2 * MXU):
                jobs.append(
                    Job(
                        mine,
                        ring.at[i % slots, :, pl.ds(start, 2 * MXU)],
                        down_copy(i).wait if start == 0 else nothing,
                        down_done(which, i, n * DOWN + start),
                        n == 0 and start == 0,
                    )
                )

    pl.run_scoped(
        lambda a, b, c, d: run_jobs(jobs, [[a, b], [c, d]]),
        *[pltpu.ACC(m)((tokens, MXU), jnp.float32) for _ in range(2) for m in range(2)],
    )


def experts(parts, w_gate, w_up, w_down, group_rows, dev_count):
    tokens = parts.shape[0]
    width, local_hidden = w_gate.shape
    columns = width // dev_count
    units = local_hidden // PASSES
    return pl.pallas_call(
        experts_kernel,
        out_shape=jax.ShapeDtypeStruct((SHARING_DEVICES * tokens, group_rows, columns), jnp.bfloat16),
        in_specs=[VMEM, VMEM, VMEM, HBM],
        out_specs=VMEM,
        scratch_shapes=[
            pltpu.VMEM((tokens * width // HEAD_SIZE, HEAD_SIZE), jnp.float32),
            pltpu.VMEM((tokens, width), jnp.bfloat16),
            pltpu.VMEM((tokens, local_hidden), jnp.bfloat16),
            pltpu.VMEM((tokens, 2 * MXU), jnp.float32),
            pltpu.VMEM((tokens, width), jnp.float32),
            pltpu.VMEM((RING, units, DOWN), jnp.bfloat16),
            pltpu.SemaphoreType.DMA((RING,)),
        ],
        compiler_params=pltpu.CompilerParams(vmem_limit_bytes=RING * units * DOWN * 2 + 2 * MIB),
        name="experts",
    )(*in_vmem(parts, w_gate, w_up), *in_hbm(w_down))


def experts_plain(parts, w_gate, w_up, w_down, group_rows, dev_count):
    width = w_gate.shape[0]
    normed = parts.reshape(-1, width)
    gate = jnp.dot(normed, w_gate, preferred_element_type=jnp.float32)
    up = jnp.dot(normed, w_up, preferred_element_type=jnp.float32)
    hidden = (jax.nn.silu(gate) * up).astype(jnp.bfloat16)
    part = jnp.dot(hidden, w_down, preferred_element_type=jnp.float32).astype(jnp.bfloat16)
    part = part.reshape(-1, group_rows, dev_count, width // dev_count)
    return part.transpose(0, 2, 1, 3).reshape(-1, group_rows, width // dev_count)


def combine_kernel(per_expert, dev_count, parts, weights, out):
    shards = parts.shape[0] // dev_count
    weight = weights[...]
    total = jnp.zeros(out.shape, jnp.float32)
    for e in range(E):
        here = jnp.zeros(out.shape, jnp.float32)
        for g in range(shards):
            for c in range(per_expert):
                here = here + parts[g * dev_count + e * per_expert + c].astype(jnp.float32)
        total = total + weight[:, e : e + 1] * here
    out[...] = total.astype(out.dtype)


def combine(parts, weights, dev_count):
    return pl.pallas_call(
        functools.partial(combine_kernel, dev_count // E, dev_count),
        out_shape=jax.ShapeDtypeStruct(parts.shape[1:], jnp.bfloat16),
        in_specs=[VMEM] * 2,
        out_specs=VMEM,
        compiler_params=pltpu.CompilerParams(vmem_limit_bytes=24 * MIB),
        name="combine",
    )(*in_vmem(parts, weights))


def body(
    queries,
    cached_key_rows,
    cached_value_rows,
    incoming_keys,
    incoming_values,
    lengths,
    residual,
    norm_gain,
    expert_ids,
    route_logits,
    w_gate,
    w_up,
    w_down,
):
    chips = lax.axis_size("grp") * lax.axis_size("pair")
    dev_count = lax.axis_size("pair") * SHARING_DEVICES
    group_rows = residual.shape[0]
    summed, weights = attend(
        lengths, queries, cached_key_rows, cached_value_rows, incoming_keys, incoming_values,
        residual, expert_ids, route_logits,
    )
    other = lax.ppermute(summed, "half", [(0, 1), (1, 0)])
    sent = norm(summed, other, norm_gain, chips)
    rows = lax.all_to_all(sent, ("grp", "pair"), 0, 0, tiled=True)
    whole_blocks = w_gate.shape[1] % (PASSES * TILE) == 0 and norm_gain.shape[0] // dev_count % PART == 0
    run_experts = experts if whole_blocks else experts_plain
    part = run_experts(rows, w_gate, w_up, w_down, group_rows, dev_count)
    got = lax.all_to_all(part, ("grp", "pair", "half"), 0, 0, tiled=True)
    return combine(got, weights, dev_count)


def solution(mesh):
    groups, dev_count = mesh.devices.shape
    split = jax.sharding.Mesh(
        mesh.devices.reshape(groups, dev_count // SHARING_DEVICES, SHARING_DEVICES),
        ("grp", "pair", "half"),
    )
    dev = ("pair", "half")
    rows = ("grp",) + dev
    shards = dev + ("grp",)
    return jax.shard_map(
        body,
        mesh=split,
        in_specs=(
            P(rows, None),
            P(rows, None, None),
            P(rows, None, None),
            P(rows, None),
            P(rows, None),
            P("grp"),
            P("grp", None),
            P(),
            P("grp", None),
            P("grp", None),
            P(None, shards),
            P(None, shards),
            P(shards, None),
        ),
        out_specs=P("grp", dev),
        check_vma=False,
    )
```

```python
import functools
import math

import jax
import jax.numpy as jnp
from jax import lax
from jax.experimental import pallas as pl
from jax.experimental.pallas import tpu as pltpu
from jax.sharding import PartitionSpec as P

QUERY_HEADS = 48
KEY_VALUE_HEADS = 8
HEAD_SIZE = 128
E = 8
SHARING_DEVICES = 2
GROUP_WIDTH = QUERY_HEADS // KEY_VALUE_HEADS
LOCAL_HEADS = QUERY_HEADS // SHARING_DEVICES
MIB = 2**20
VMEM = pl.BlockSpec(memory_space=pltpu.VMEM)
HBM = pl.BlockSpec(memory_space=pltpu.HBM)
MXU = 256
TILE = 512
PART = 256
RING = 6
PASSES = 2
DOWN = 1024
UNTIL_ROWS = pl.CostEstimate(flops=40_000_000_000, bytes_accessed=0, transcendentals=0)


def in_hbm(*arrays):
    return [pltpu.with_memory_space_constraint(a, pltpu.HBM) for a in arrays]


def in_vmem(*arrays):
    return [pltpu.with_memory_space_constraint(a, pltpu.VMEM) for a in arrays]


def head_rows(row):
    heads = row.shape[1] // HEAD_SIZE
    return jnp.concatenate(
        [row[:, j * HEAD_SIZE : (j + 1) * HEAD_SIZE] for j in range(heads)], axis=0
    )


def as_column(row, diagonal):
    return jnp.sum(jnp.where(diagonal, row, jnp.zeros_like(row)), axis=1, keepdims=True)


def attend_kernel(
    lengths, queries, key_rows, value_rows, new_keys, new_values, residual, ids, logits, out, weights_out,
    length_buf, query_buf, key_buf, value_buf, new_key_buf, new_value_buf, residual_buf, id_buf, logit_buf,
    sems,
):
    sequence, half = lax.axis_index("pair"), lax.axis_index("half")
    heads = LOCAL_HEADS
    columns = heads * HEAD_SIZE
    at = pl.ds(pl.multiple_of(half * columns, HEAD_SIZE), columns)
    pairs = [
        (key_rows.at[0], key_buf),
        (queries, query_buf),
        (new_keys, new_key_buf),
        (lengths, length_buf),
        (new_values, new_value_buf),
        (value_rows.at[0], value_buf),
        (residual.at[:, at], residual_buf),
        (ids, id_buf),
        (logits, logit_buf),
    ]
    copies = [pltpu.make_async_copy(*pair, sems.at[i]) for i, pair in enumerate(pairs)]
    for copy in copies:
        copy.start()
    cache_len, width = key_buf.shape
    kv_heads = width // HEAD_SIZE
    scale = HEAD_SIZE ** (-0.5)
    for copy in copies[:4]:
        copy.wait()
    query = head_rows(query_buf[...].astype(jnp.float32))
    owner = lax.broadcasted_iota(jnp.int32, (heads, HEAD_SIZE), 0) // GROUP_WIDTH
    blocks = [jnp.where(owner == b, query, 0.0) for b in range(kv_heads)]
    spread = jnp.concatenate(blocks, axis=1)
    scores = (
        lax.dot_general(
            spread.astype(jnp.bfloat16),
            key_buf[...],
            (((1,), (1,)), ((), ())),
            preferred_element_type=jnp.float32,
        )
        * scale
    )
    places = lax.broadcasted_iota(jnp.int32, (heads, cache_len), 1)
    scores = jnp.where(places < length_buf[sequence], scores, -1e30)
    new_score = (
        jnp.sum(spread * new_key_buf[...].astype(jnp.float32), axis=1, keepdims=True) * scale
    )
    row_max = jnp.maximum(jnp.max(scores, axis=1, keepdims=True), new_score)
    exp_all = jnp.exp(scores - row_max)
    exp_new = jnp.exp(new_score - row_max)
    denom = jnp.sum(exp_all, axis=1, keepdims=True) + exp_new
    weights = (exp_all / denom).astype(jnp.bfloat16)
    weight_new = (exp_new / denom).astype(jnp.bfloat16).astype(jnp.float32)
    for copy in copies[4:]:
        copy.wait()
    mixed = jnp.dot(weights, value_buf[...], preferred_element_type=jnp.float32)
    mixed = mixed + weight_new * new_value_buf[...].astype(jnp.float32)
    attended = jnp.zeros((heads, HEAD_SIZE), jnp.float32)
    for b in range(kv_heads):
        attended = jnp.where(
            owner == b, mixed[:, b * HEAD_SIZE : (b + 1) * HEAD_SIZE], attended
        )
    attended = attended.astype(jnp.bfloat16).astype(jnp.float32)
    mine = residual_buf[...].astype(jnp.float32)
    rows = lax.broadcasted_iota(jnp.int32, mine.shape, 0)
    mine = jnp.sum(jnp.where(rows == sequence, mine, 0.0), axis=0, keepdims=True)
    out[...] = attended + head_rows(mine)

    count, tokens = id_buf.shape
    diagonal = lax.broadcasted_iota(jnp.int32, (tokens, tokens), 0) == lax.broadcasted_iota(
        jnp.int32, (tokens, tokens), 1
    )
    chosen = [as_column(id_buf[k : k + 1, :], diagonal) for k in range(count)]
    logit = [as_column(logit_buf[k : k + 1, :], diagonal) for k in range(count)]
    top = functools.reduce(jnp.maximum, logit)
    raised = [jnp.exp(v - top) for v in logit]
    scale = 1.0 / functools.reduce(jnp.add, raised)
    expert = lax.broadcasted_iota(jnp.int32, weights_out.shape, 1)
    by_expert = jnp.zeros(weights_out.shape, jnp.float32)
    for k in range(count):
        by_expert = by_expert + jnp.where(chosen[k] == expert, raised[k] * scale, 0.0)
    weights_out[...] = by_expert


def attend(lengths, queries, key_rows, value_rows, new_keys, new_values, residual, ids, logits):
    half_columns = LOCAL_HEADS * HEAD_SIZE
    operands = [lengths, queries, key_rows, value_rows, new_keys, new_values, residual, ids.T, logits.T]
    return pl.pallas_call(
        attend_kernel,
        out_shape=(
            jax.ShapeDtypeStruct((LOCAL_HEADS, HEAD_SIZE), jnp.float32),
            jax.ShapeDtypeStruct((ids.shape[0], E), jnp.float32),
        ),
        in_specs=[HBM] * len(operands),
        out_specs=(VMEM, VMEM),
        scratch_shapes=[
            pltpu.SMEM(lengths.shape, jnp.int32),
            pltpu.VMEM(queries.shape, jnp.bfloat16),
            pltpu.VMEM(key_rows.shape[1:], jnp.bfloat16),
            pltpu.VMEM(value_rows.shape[1:], jnp.bfloat16),
            pltpu.VMEM(new_keys.shape, jnp.bfloat16),
            pltpu.VMEM(new_values.shape, jnp.bfloat16),
            pltpu.VMEM((residual.shape[0], half_columns), jnp.bfloat16),
            pltpu.VMEM(ids.shape[::-1], jnp.int32),
            pltpu.VMEM(logits.shape[::-1], jnp.float32),
            pltpu.SemaphoreType.DMA((len(operands),)),
        ],
        compiler_params=pltpu.CompilerParams(vmem_limit_bytes=4 * MIB),
        cost_estimate=UNTIL_ROWS,
        name="attend",
    )(*in_hbm(*operands))


def norm_kernel(mine, other, gain, out):
    heads = mine.shape[0]
    own = mine[...]
    square = jnp.sum(own * own + other[...] * other[...], axis=0, keepdims=True)
    square = jnp.sum(square, axis=1, keepdims=True)
    inverse = lax.rsqrt(square * (1.0 / (SHARING_DEVICES * heads * HEAD_SIZE)) + 1e-05)
    at = pl.ds(pl.multiple_of(lax.axis_index("half") * heads, 8), heads)
    normed = (own * inverse * gain[at, :]).astype(jnp.bfloat16)
    out[...] = jnp.broadcast_to(normed[None], out.shape)


def norm(mine, other, gain, devices):
    shape = (devices,) + mine.shape
    return pl.pallas_call(
        norm_kernel,
        out_shape=jax.ShapeDtypeStruct(shape, jnp.bfloat16),
        in_specs=[VMEM] * 3,
        out_specs=VMEM,
        compiler_params=pltpu.CompilerParams(vmem_limit_bytes=MIB + 2 * math.prod(shape)),
        name="norm",
    )(mine, other, gain.reshape(-1, HEAD_SIZE))


class Job:
    def __init__(self, rows, weight, before, after, after_rows):
        self.rows, self.weight, self.before, self.after = rows, weight, before, after
        self.after_rows = after_rows


def run_jobs(jobs, sums):
    steps = [(n, k) for n, job in enumerate(jobs) for k in range(0, job.rows.shape[1], MXU)]

    def push(i):
        n, k = steps[i]
        job = jobs[n]
        if k == 0:
            job.before()
        for m in range(2):
            tile = job.weight[k : k + MXU, m * MXU : (m + 1) * MXU]
            pltpu.matmul_push_rhs(tile, i % 2, m)

    pending = []

    def settle():
        while pending:
            n = pending.pop()
            jobs[n].after([pltpu.matmul_pop(sums[n % 2][m]) for m in range(2)])

    push(0)
    for i, (n, k) in enumerate(steps):
        if i + 1 < len(steps):
            push(i + 1)
        job = jobs[n]
        if k == 0 and job.after_rows:
            settle()
        for m in range(2):
            pltpu.matmul_acc_lhs(sums[n % 2][m], job.rows[:, k : k + MXU], load_staged_rhs=i % 2)
        settle()
        if k + MXU == job.rows.shape[1]:
            pending.append(n)
    settle()


def experts_kernel(
    parts, w_gate, w_up, w_down, out, flat, normed, hidden, gates, total, ring, sems
):
    tokens, width = normed.shape
    slots, units = ring.shape[:2]
    heads = width // HEAD_SIZE
    group_rows, columns = out.shape[1:]
    targets = width // columns
    blocks = width // DOWN

    def down_copy(i):
        which, n = divmod(i, blocks)
        source = w_down.at[pl.ds(which * units, units), pl.ds(n * DOWN, DOWN)]
        return pltpu.make_async_copy(source, ring.at[i % slots], sems.at[i % slots])

    for i in range(min(slots, PASSES * blocks)):
        down_copy(i).start()

    flat[...] = parts[...].astype(jnp.float32).reshape(flat.shape)
    for j in range(heads):
        normed[:, j * HEAD_SIZE : (j + 1) * HEAD_SIZE] = flat[
            pl.ds(j, tokens, stride=heads), :
        ].astype(jnp.bfloat16)

    def nothing():
        pass

    def gate_done(start):
        def after(sums):
            for m in range(2):
                gates[:, m * MXU : (m + 1) * MXU] = sums[m]

        return after

    def up_done(start):
        def after(sums):
            for m in range(2):
                gate = gates[:, m * MXU : (m + 1) * MXU]
                at = slice(start + m * MXU, start + (m + 1) * MXU)
                hidden[:, at] = (gate / (1.0 + jnp.exp(-gate)) * sums[m]).astype(jnp.bfloat16)

        return after

    def down_done(which, i, start):
        def after(sums):
            for m in range(2):
                column = start + m * MXU
                part = sums[m]
                at = slice(column, column + MXU)
                if which > 0:
                    part = total[:, at] + part
                if which < PASSES - 1:
                    total[:, at] = part
                    continue
                target, place = divmod(column, columns)
                for g in range(tokens // group_rows):
                    out[g * targets + target, :, place : place + MXU] = part[
                        g * group_rows : (g + 1) * group_rows
                    ].astype(out.dtype)
            if (start + 2 * MXU) % DOWN == 0 and i + slots < PASSES * blocks:
                down_copy(i + slots).start()

        return after

    jobs = []
    for which in range(PASSES):
        for start in range(which * units, (which + 1) * units, 2 * MXU):
            at = pl.ds(start, 2 * MXU)
            jobs.append(Job(normed, w_gate.at[:, at], nothing, gate_done(start), False))
            jobs.append(Job(normed, w_up.at[:, at], nothing, up_done(start), False))
        mine = hidden.at[:, pl.ds(which * units, units)]
        for n in range(blocks):
            i = which * blocks + n
            for start in range(0, DOWN, 2 * MXU):
                jobs.append(
                    Job(
                        mine,
                        ring.at[i % slots, :, pl.ds(start, 2 * MXU)],
                        down_copy(i).wait if start == 0 else nothing,
                        down_done(which, i, n * DOWN + start),
                        n == 0 and start == 0,
                    )
                )

    pl.run_scoped(
        lambda a, b, c, d: run_jobs(jobs, [[a, b], [c, d]]),
        *[pltpu.ACC(m)((tokens, MXU), jnp.float32) for _ in range(2) for m in range(2)],
    )


def experts(parts, w_gate, w_up, w_down, group_rows, dev_count):
    devices = parts.shape[0]
    width, local_hidden = w_gate.shape
    tokens = devices // SHARING_DEVICES
    columns = width // dev_count
    units = local_hidden // PASSES
    return pl.pallas_call(
        experts_kernel,
        out_shape=jax.ShapeDtypeStruct((devices, group_rows, columns), jnp.bfloat16),
        in_specs=[VMEM, VMEM, VMEM, HBM],
        out_specs=VMEM,
        scratch_shapes=[
            pltpu.VMEM((tokens * width // HEAD_SIZE, HEAD_SIZE), jnp.float32),
            pltpu.VMEM((tokens, width), jnp.bfloat16),
            pltpu.VMEM((tokens, local_hidden), jnp.bfloat16),
            pltpu.VMEM((tokens, 2 * MXU), jnp.float32),
            pltpu.VMEM((tokens, width), jnp.float32),
            pltpu.VMEM((RING, units, DOWN), jnp.bfloat16),
            pltpu.SemaphoreType.DMA((RING,)),
        ],
        compiler_params=pltpu.CompilerParams(vmem_limit_bytes=RING * units * DOWN * 2 + 2 * MIB),
        name="experts",
    )(*in_vmem(parts, w_gate, w_up), *in_hbm(w_down))


def experts_plain(parts, w_gate, w_up, w_down, group_rows, dev_count):
    width = w_gate.shape[0]
    normed = parts.reshape(-1, width)
    gate = jnp.dot(normed, w_gate, preferred_element_type=jnp.float32)
    up = jnp.dot(normed, w_up, preferred_element_type=jnp.float32)
    hidden = (jax.nn.silu(gate) * up).astype(jnp.bfloat16)
    part = jnp.dot(hidden, w_down, preferred_element_type=jnp.float32).astype(jnp.bfloat16)
    part = part.reshape(-1, group_rows, dev_count, width // dev_count)
    return part.transpose(0, 2, 1, 3).reshape(-1, group_rows, width // dev_count)


def combine_kernel(per_expert, dev_count, parts, weights, out):
    shards = parts.shape[0] // dev_count
    weight = weights[...]
    total = jnp.zeros(out.shape, jnp.float32)
    for e in range(E):
        here = jnp.zeros(out.shape, jnp.float32)
        for g in range(shards):
            for c in range(per_expert):
                here = here + parts[g * dev_count + e * per_expert + c].astype(jnp.float32)
        total = total + weight[:, e : e + 1] * here
    out[...] = total.astype(out.dtype)


def combine(parts, weights, dev_count):
    return pl.pallas_call(
        functools.partial(combine_kernel, dev_count // E, dev_count),
        out_shape=jax.ShapeDtypeStruct(parts.shape[1:], jnp.bfloat16),
        in_specs=[VMEM] * 2,
        out_specs=VMEM,
        compiler_params=pltpu.CompilerParams(vmem_limit_bytes=24 * MIB),
        name="combine",
    )(*in_vmem(parts, weights))


def body(
    queries,
    cached_key_rows,
    cached_value_rows,
    incoming_keys,
    incoming_values,
    lengths,
    residual,
    norm_gain,
    expert_ids,
    route_logits,
    w_gate,
    w_up,
    w_down,
):
    dev_count = lax.axis_size("pair") * SHARING_DEVICES
    group_rows = residual.shape[0]
    summed, weights = attend(
        lengths, queries, cached_key_rows, cached_value_rows, incoming_keys, incoming_values,
        residual, expert_ids, route_logits,
    )
    other = lax.ppermute(summed, "half", [(0, 1), (1, 0)])
    sent = norm(summed, other, norm_gain, lax.axis_size("grp") * dev_count)
    rows = lax.all_to_all(sent, ("grp", "pair", "half"), 0, 0, tiled=True)
    whole_blocks = w_gate.shape[1] % (PASSES * TILE) == 0 and norm_gain.shape[0] // dev_count % PART == 0
    run_experts = experts if whole_blocks else experts_plain
    part = run_experts(rows, w_gate, w_up, w_down, group_rows, dev_count)
    got = lax.all_to_all(part, ("grp", "pair", "half"), 0, 0, tiled=True)
    return combine(got, weights, dev_count)


def solution(mesh):
    groups, dev_count = mesh.devices.shape
    split = jax.sharding.Mesh(
        mesh.devices.reshape(groups, dev_count // SHARING_DEVICES, SHARING_DEVICES),
        ("grp", "pair", "half"),
    )
    dev = ("pair", "half")
    rows = ("grp",) + dev
    shards = dev + ("grp",)
    return jax.shard_map(
        body,
        mesh=split,
        in_specs=(
            P(rows, None),
            P(rows, None, None),
            P(rows, None, None),
            P(rows, None),
            P(rows, None),
            P("grp"),
            P("grp", None),
            P(),
            P("grp", None),
            P("grp", None),
            P(None, shards),
            P(None, shards),
            P(shards, None),
        ),
        out_specs=P("grp", dev),
        check_vma=False,
    )
```

```python
import functools
import math

import jax
import jax.numpy as jnp
from jax import lax
from jax.experimental import pallas as pl
from jax.experimental.pallas import tpu as pltpu
from jax.sharding import PartitionSpec as P

QUERY_HEADS = 48
KEY_VALUE_HEADS = 8
HEAD_SIZE = 128
E = 8
SHARING_DEVICES = 2
GROUP_WIDTH = QUERY_HEADS // KEY_VALUE_HEADS
LOCAL_HEADS = QUERY_HEADS // SHARING_DEVICES
MIB = 2**20
VMEM = pl.BlockSpec(memory_space=pltpu.VMEM)
HBM = pl.BlockSpec(memory_space=pltpu.HBM)
MXU = 256
TILE = 512
PART = 256
RING = 6
PASSES = 2
DOWN = 1024
UNTIL_ROWS = pl.CostEstimate(flops=40_000_000_000, bytes_accessed=0, transcendentals=0)


def in_hbm(*arrays):
    return [pltpu.with_memory_space_constraint(a, pltpu.HBM) for a in arrays]


def in_vmem(*arrays):
    return [pltpu.with_memory_space_constraint(a, pltpu.VMEM) for a in arrays]


def head_rows(row):
    heads = row.shape[1] // HEAD_SIZE
    return jnp.concatenate(
        [row[:, j * HEAD_SIZE : (j + 1) * HEAD_SIZE] for j in range(heads)], axis=0
    )


def as_column(row, diagonal):
    return jnp.sum(jnp.where(diagonal, row, jnp.zeros_like(row)), axis=1, keepdims=True)


def attend_kernel(
    lengths, queries, key_rows, value_rows, new_keys, new_values, residual, ids, logits, out, weights_out,
    length_buf, query_buf, key_buf, value_buf, new_key_buf, new_value_buf, residual_buf, id_buf, logit_buf,
    sems,
):
    sequence, half = lax.axis_index("pair"), lax.axis_index("half")
    heads = LOCAL_HEADS
    columns = heads * HEAD_SIZE
    at = pl.ds(pl.multiple_of(half * columns, HEAD_SIZE), columns)
    pairs = [
        (key_rows.at[0], key_buf),
        (queries, query_buf),
        (new_keys, new_key_buf),
        (lengths, length_buf),
        (new_values, new_value_buf),
        (value_rows.at[0], value_buf),
        (residual.at[:, at], residual_buf),
        (ids, id_buf),
        (logits, logit_buf),
    ]
    copies = [pltpu.make_async_copy(*pair, sems.at[i]) for i, pair in enumerate(pairs)]
    for copy in copies:
        copy.start()
    cache_len, width = key_buf.shape
    kv_heads = width // HEAD_SIZE
    scale = HEAD_SIZE ** (-0.5)
    for copy in copies[:4]:
        copy.wait()
    query = head_rows(query_buf[...].astype(jnp.float32))
    owner = lax.broadcasted_iota(jnp.int32, (heads, HEAD_SIZE), 0) // GROUP_WIDTH
    blocks = [jnp.where(owner == b, query, 0.0) for b in range(kv_heads)]
    spread = jnp.concatenate(blocks, axis=1)
    scores = (
        lax.dot_general(
            spread.astype(jnp.bfloat16),
            key_buf[...],
            (((1,), (1,)), ((), ())),
            preferred_element_type=jnp.float32,
        )
        * scale
    )
    places = lax.broadcasted_iota(jnp.int32, (heads, cache_len), 1)
    scores = jnp.where(places < length_buf[sequence], scores, -1e30)
    new_score = (
        jnp.sum(spread * new_key_buf[...].astype(jnp.float32), axis=1, keepdims=True) * scale
    )
    row_max = jnp.maximum(jnp.max(scores, axis=1, keepdims=True), new_score)
    exp_all = jnp.exp(scores - row_max)
    exp_new = jnp.exp(new_score - row_max)
    denom = jnp.sum(exp_all, axis=1, keepdims=True) + exp_new
    weights = (exp_all / denom).astype(jnp.bfloat16)
    weight_new = (exp_new / denom).astype(jnp.bfloat16).astype(jnp.float32)
    for copy in copies[4:]:
        copy.wait()
    mixed = jnp.dot(weights, value_buf[...], preferred_element_type=jnp.float32)
    mixed = mixed + weight_new * new_value_buf[...].astype(jnp.float32)
    attended = jnp.zeros((heads, HEAD_SIZE), jnp.float32)
    for b in range(kv_heads):
        attended = jnp.where(
            owner == b, mixed[:, b * HEAD_SIZE : (b + 1) * HEAD_SIZE], attended
        )
    attended = attended.astype(jnp.bfloat16).astype(jnp.float32)
    mine = residual_buf[...].astype(jnp.float32)
    rows = lax.broadcasted_iota(jnp.int32, mine.shape, 0)
    mine = jnp.sum(jnp.where(rows == sequence, mine, 0.0), axis=0, keepdims=True)
    out[...] = attended + head_rows(mine)

    count, tokens = id_buf.shape
    diagonal = lax.broadcasted_iota(jnp.int32, (tokens, tokens), 0) == lax.broadcasted_iota(
        jnp.int32, (tokens, tokens), 1
    )
    chosen = [as_column(id_buf[k : k + 1, :], diagonal) for k in range(count)]
    logit = [as_column(logit_buf[k : k + 1, :], diagonal) for k in range(count)]
    top = functools.reduce(jnp.maximum, logit)
    raised = [jnp.exp(v - top) for v in logit]
    scale = 1.0 / functools.reduce(jnp.add, raised)
    expert = lax.broadcasted_iota(jnp.int32, weights_out.shape, 1)
    by_expert = jnp.zeros(weights_out.shape, jnp.float32)
    for k in range(count):
        by_expert = by_expert + jnp.where(chosen[k] == expert, raised[k] * scale, 0.0)
    weights_out[...] = by_expert


def attend(lengths, queries, key_rows, value_rows, new_keys, new_values, residual, ids, logits):
    half_columns = LOCAL_HEADS * HEAD_SIZE
    operands = [lengths, queries, key_rows, value_rows, new_keys, new_values, residual, ids.T, logits.T]
    return pl.pallas_call(
        attend_kernel,
        out_shape=(
            jax.ShapeDtypeStruct((LOCAL_HEADS, HEAD_SIZE), jnp.float32),
            jax.ShapeDtypeStruct((ids.shape[0], E), jnp.float32),
        ),
        in_specs=[HBM] * len(operands),
        out_specs=(VMEM, VMEM),
        scratch_shapes=[
            pltpu.SMEM(lengths.shape, jnp.int32),
            pltpu.VMEM(queries.shape, jnp.bfloat16),
            pltpu.VMEM(key_rows.shape[1:], jnp.bfloat16),
            pltpu.VMEM(value_rows.shape[1:], jnp.bfloat16),
            pltpu.VMEM(new_keys.shape, jnp.bfloat16),
            pltpu.VMEM(new_values.shape, jnp.bfloat16),
            pltpu.VMEM((residual.shape[0], half_columns), jnp.bfloat16),
            pltpu.VMEM(ids.shape[::-1], jnp.int32),
            pltpu.VMEM(logits.shape[::-1], jnp.float32),
            pltpu.SemaphoreType.DMA((len(operands),)),
        ],
        compiler_params=pltpu.CompilerParams(vmem_limit_bytes=4 * MIB),
        cost_estimate=UNTIL_ROWS,
        name="attend",
    )(*in_hbm(*operands))


def norm_kernel(mine, other, gain, out):
    heads = mine.shape[0]
    own = mine[...]
    square = jnp.sum(own * own + other[...] * other[...], axis=0, keepdims=True)
    square = jnp.sum(square, axis=1, keepdims=True)
    inverse = lax.rsqrt(square * (1.0 / (SHARING_DEVICES * heads * HEAD_SIZE)) + 1e-05)
    at = pl.ds(pl.multiple_of(lax.axis_index("half") * heads, 8), heads)
    normed = (own * inverse * gain[at, :]).astype(jnp.bfloat16)
    out[...] = jnp.broadcast_to(normed[None], out.shape)


def norm(mine, other, gain, devices):
    shape = (devices,) + mine.shape
    return pl.pallas_call(
        norm_kernel,
        out_shape=jax.ShapeDtypeStruct(shape, jnp.bfloat16),
        in_specs=[VMEM] * 3,
        out_specs=VMEM,
        compiler_params=pltpu.CompilerParams(vmem_limit_bytes=MIB + 2 * math.prod(shape)),
        name="norm",
    )(mine, other, gain.reshape(-1, HEAD_SIZE))


class Job:
    def __init__(self, rows, weight, before, after, after_rows):
        self.rows, self.weight, self.before, self.after = rows, weight, before, after
        self.after_rows = after_rows


def run_jobs(jobs, sums):
    steps = [(n, k) for n, job in enumerate(jobs) for k in range(0, job.rows.shape[1], MXU)]

    def push(i):
        n, k = steps[i]
        job = jobs[n]
        if k == 0:
            job.before()
        for m in range(2):
            tile = job.weight[k : k + MXU, m * MXU : (m + 1) * MXU]
            pltpu.matmul_push_rhs(tile, i % 2, m)

    pending = []

    def settle():
        while pending:
            n = pending.pop()
            jobs[n].after([pltpu.matmul_pop(sums[n % 2][m]) for m in range(2)])

    push(0)
    for i, (n, k) in enumerate(steps):
        if i + 1 < len(steps):
            push(i + 1)
        job = jobs[n]
        if k == 0 and job.after_rows:
            settle()
        for m in range(2):
            pltpu.matmul_acc_lhs(sums[n % 2][m], job.rows[:, k : k + MXU], load_staged_rhs=i % 2)
        settle()
        if k + MXU == job.rows.shape[1]:
            pending.append(n)
    settle()


def experts_kernel(
    parts, w_gate, w_up, w_down, out, flat, normed, hidden, gates, total, ring, sems
):
    tokens, width = normed.shape
    slots, units = ring.shape[:2]
    heads = width // HEAD_SIZE
    group_rows, columns = out.shape[1:]
    targets = width // columns
    blocks = width // DOWN

    def down_copy(i):
        which, n = divmod(i, blocks)
        source = w_down.at[pl.ds(which * units, units), pl.ds(n * DOWN, DOWN)]
        return pltpu.make_async_copy(source, ring.at[i % slots], sems.at[i % slots])

    for i in range(min(slots, PASSES * blocks)):
        down_copy(i).start()

    flat[...] = parts[...].astype(jnp.float32).reshape(flat.shape)
    for j in range(heads):
        normed[:, j * HEAD_SIZE : (j + 1) * HEAD_SIZE] = flat[
            pl.ds(j, tokens, stride=heads), :
        ].astype(jnp.bfloat16)

    def nothing():
        pass

    def gate_done(start):
        def after(sums):
            for m in range(2):
                gates[:, m * MXU : (m + 1) * MXU] = sums[m]

        return after

    def up_done(start):
        def after(sums):
            for m in range(2):
                gate = gates[:, m * MXU : (m + 1) * MXU]
                at = slice(start + m * MXU, start + (m + 1) * MXU)
                hidden[:, at] = (gate / (1.0 + jnp.exp(-gate)) * sums[m]).astype(jnp.bfloat16)

        return after

    def down_done(which, i, start):
        def after(sums):
            for m in range(2):
                column = start + m * MXU
                part = sums[m]
                at = slice(column, column + MXU)
                if which > 0:
                    part = total[:, at] + part
                if which < PASSES - 1:
                    total[:, at] = part
                    continue
                target, place = divmod(column, columns)
                for g in range(tokens // group_rows):
                    out[g * targets + target, :, place : place + MXU] = part[
                        g * group_rows : (g + 1) * group_rows
                    ].astype(out.dtype)
            if (start + 2 * MXU) % DOWN == 0 and i + slots < PASSES * blocks:
                down_copy(i + slots).start()

        return after

    jobs = []
    for which in range(PASSES):
        for start in range(which * units, (which + 1) * units, 2 * MXU):
            at = pl.ds(start, 2 * MXU)
            jobs.append(Job(normed, w_gate.at[:, at], nothing, gate_done(start), False))
            jobs.append(Job(normed, w_up.at[:, at], nothing, up_done(start), False))
        mine = hidden.at[:, pl.ds(which * units, units)]
        for n in range(blocks):
            i = which * blocks + n
            for start in range(0, DOWN, 2 * MXU):
                jobs.append(
                    Job(
                        mine,
                        ring.at[i % slots, :, pl.ds(start, 2 * MXU)],
                        down_copy(i).wait if start == 0 else nothing,
                        down_done(which, i, n * DOWN + start),
                        n == 0 and start == 0,
                    )
                )

    pl.run_scoped(
        lambda a, b, c, d: run_jobs(jobs, [[a, b], [c, d]]),
        *[pltpu.ACC(m)((tokens, MXU), jnp.float32) for _ in range(2) for m in range(2)],
    )


def experts(parts, w_gate, w_up, w_down, group_rows, dev_count):
    devices = parts.shape[0]
    width, local_hidden = w_gate.shape
    tokens = devices // SHARING_DEVICES
    columns = width // dev_count
    units = local_hidden // PASSES
    return pl.pallas_call(
        experts_kernel,
        out_shape=pltpu.VMEM((devices, group_rows, columns), jnp.bfloat16),
        in_specs=[VMEM, VMEM, VMEM, HBM],
        out_specs=VMEM,
        scratch_shapes=[
            pltpu.VMEM((tokens * width // HEAD_SIZE, HEAD_SIZE), jnp.float32),
            pltpu.VMEM((tokens, width), jnp.bfloat16),
            pltpu.VMEM((tokens, local_hidden), jnp.bfloat16),
            pltpu.VMEM((tokens, 2 * MXU), jnp.float32),
            pltpu.VMEM((tokens, width), jnp.float32),
            pltpu.VMEM((RING, units, DOWN), jnp.bfloat16),
            pltpu.SemaphoreType.DMA((RING,)),
        ],
        compiler_params=pltpu.CompilerParams(vmem_limit_bytes=RING * units * DOWN * 2 + 2 * MIB),
        name="experts",
    )(*in_vmem(parts, w_gate, w_up), *in_hbm(w_down))


def experts_plain(parts, w_gate, w_up, w_down, group_rows, dev_count):
    width = w_gate.shape[0]
    normed = parts.reshape(-1, width)
    gate = jnp.dot(normed, w_gate, preferred_element_type=jnp.float32)
    up = jnp.dot(normed, w_up, preferred_element_type=jnp.float32)
    hidden = (jax.nn.silu(gate) * up).astype(jnp.bfloat16)
    part = jnp.dot(hidden, w_down, preferred_element_type=jnp.float32).astype(jnp.bfloat16)
    part = part.reshape(-1, group_rows, dev_count, width // dev_count)
    return part.transpose(0, 2, 1, 3).reshape(-1, group_rows, width // dev_count)


def combine_kernel(per_expert, dev_count, parts, weights, out):
    shards = parts.shape[0] // dev_count
    weight = weights[...]
    total = jnp.zeros(out.shape, jnp.float32)
    for e in range(E):
        here = jnp.zeros(out.shape, jnp.float32)
        for g in range(shards):
            for c in range(per_expert):
                here = here + parts[g * dev_count + e * per_expert + c].astype(jnp.float32)
        total = total + weight[:, e : e + 1] * here
    out[...] = total.astype(out.dtype)


def combine(parts, weights, dev_count):
    return pl.pallas_call(
        functools.partial(combine_kernel, dev_count // E, dev_count),
        out_shape=jax.ShapeDtypeStruct(parts.shape[1:], jnp.bfloat16),
        in_specs=[VMEM] * 2,
        out_specs=VMEM,
        compiler_params=pltpu.CompilerParams(vmem_limit_bytes=24 * MIB),
        name="combine",
    )(*in_vmem(parts, weights))


def body(
    queries,
    cached_key_rows,
    cached_value_rows,
    incoming_keys,
    incoming_values,
    lengths,
    residual,
    norm_gain,
    expert_ids,
    route_logits,
    w_gate,
    w_up,
    w_down,
):
    dev_count = lax.axis_size("pair") * SHARING_DEVICES
    group_rows = residual.shape[0]
    summed, weights = attend(
        lengths, queries, cached_key_rows, cached_value_rows, incoming_keys, incoming_values,
        residual, expert_ids, route_logits,
    )
    other = lax.ppermute(summed, "half", [(0, 1), (1, 0)])
    sent = norm(summed, other, norm_gain, lax.axis_size("grp") * dev_count)
    rows = lax.all_to_all(sent, ("grp", "pair", "half"), 0, 0, tiled=True)
    whole_blocks = w_gate.shape[1] % (PASSES * TILE) == 0 and norm_gain.shape[0] // dev_count % PART == 0
    run_experts = experts if whole_blocks else experts_plain
    part = run_experts(rows, w_gate, w_up, w_down, group_rows, dev_count)
    got = lax.all_to_all(part, ("grp", "pair", "half"), 0, 0, tiled=True)
    return combine(got, weights, dev_count)


def solution(mesh):
    groups, dev_count = mesh.devices.shape
    split = jax.sharding.Mesh(
        mesh.devices.reshape(groups, dev_count // SHARING_DEVICES, SHARING_DEVICES),
        ("grp", "pair", "half"),
    )
    dev = ("pair", "half")
    rows = ("grp",) + dev
    shards = dev + ("grp",)
    return jax.shard_map(
        body,
        mesh=split,
        in_specs=(
            P(rows, None),
            P(rows, None, None),
            P(rows, None, None),
            P(rows, None),
            P(rows, None),
            P("grp"),
            P("grp", None),
            P(),
            P("grp", None),
            P("grp", None),
            P(None, shards),
            P(None, shards),
            P(shards, None),
        ),
        out_specs=P("grp", dev),
        check_vma=False,
    )
```

```python
import functools
import math

import jax
import jax.numpy as jnp
from jax import lax
from jax.experimental import pallas as pl
from jax.experimental.pallas import tpu as pltpu
from jax.sharding import PartitionSpec as P

QUERY_HEADS = 48
KEY_VALUE_HEADS = 8
HEAD_SIZE = 128
E = 8
SHARING_DEVICES = 2
GROUP_WIDTH = QUERY_HEADS // KEY_VALUE_HEADS
LOCAL_HEADS = QUERY_HEADS // SHARING_DEVICES
MIB = 2**20
VMEM = pl.BlockSpec(memory_space=pltpu.VMEM)
HBM = pl.BlockSpec(memory_space=pltpu.HBM)
MXU = 256
TILE = 512
PART = 256
RING = 6
PASSES = 2
DOWN = 1024
UNTIL_ROWS = pl.CostEstimate(flops=40_000_000_000, bytes_accessed=0, transcendentals=0)


def in_hbm(*arrays):
    return [pltpu.with_memory_space_constraint(a, pltpu.HBM) for a in arrays]


def in_vmem(*arrays):
    return [pltpu.with_memory_space_constraint(a, pltpu.VMEM) for a in arrays]


def head_rows(row):
    heads = row.shape[1] // HEAD_SIZE
    return jnp.concatenate(
        [row[:, j * HEAD_SIZE : (j + 1) * HEAD_SIZE] for j in range(heads)], axis=0
    )


def as_column(row, diagonal):
    return jnp.sum(jnp.where(diagonal, row, jnp.zeros_like(row)), axis=1, keepdims=True)


def attend_kernel(
    lengths, queries, key_rows, value_rows, new_keys, new_values, residual, ids, logits, out, weights_out,
    length_buf, query_buf, key_buf, value_buf, new_key_buf, new_value_buf, residual_buf, id_buf, logit_buf,
    sems,
):
    sequence, half = lax.axis_index("pair"), lax.axis_index("half")
    heads = LOCAL_HEADS
    columns = heads * HEAD_SIZE
    at = pl.ds(pl.multiple_of(half * columns, HEAD_SIZE), columns)
    pairs = [
        (key_rows.at[0], key_buf),
        (queries, query_buf),
        (new_keys, new_key_buf),
        (lengths, length_buf),
        (new_values, new_value_buf),
        (value_rows.at[0], value_buf),
        (residual.at[:, at], residual_buf),
        (ids, id_buf),
        (logits, logit_buf),
    ]
    copies = [pltpu.make_async_copy(*pair, sems.at[i]) for i, pair in enumerate(pairs)]
    for copy in copies:
        copy.start()
    cache_len, width = key_buf.shape
    kv_heads = width // HEAD_SIZE
    scale = HEAD_SIZE ** (-0.5)
    for copy in copies[:4]:
        copy.wait()
    query = head_rows(query_buf[...].astype(jnp.float32))
    owner = lax.broadcasted_iota(jnp.int32, (heads, HEAD_SIZE), 0) // GROUP_WIDTH
    blocks = [jnp.where(owner == b, query, 0.0) for b in range(kv_heads)]
    spread = jnp.concatenate(blocks, axis=1)
    scores = (
        lax.dot_general(
            spread.astype(jnp.bfloat16),
            key_buf[...],
            (((1,), (1,)), ((), ())),
            preferred_element_type=jnp.float32,
        )
        * scale
    )
    places = lax.broadcasted_iota(jnp.int32, (heads, cache_len), 1)
    scores = jnp.where(places < length_buf[sequence], scores, -1e30)
    new_score = (
        jnp.sum(spread * new_key_buf[...].astype(jnp.float32), axis=1, keepdims=True) * scale
    )
    row_max = jnp.maximum(jnp.max(scores, axis=1, keepdims=True), new_score)
    exp_all = jnp.exp(scores - row_max)
    exp_new = jnp.exp(new_score - row_max)
    denom = jnp.sum(exp_all, axis=1, keepdims=True) + exp_new
    weights = (exp_all / denom).astype(jnp.bfloat16)
    weight_new = (exp_new / denom).astype(jnp.bfloat16).astype(jnp.float32)
    for copy in copies[4:]:
        copy.wait()
    mixed = jnp.dot(weights, value_buf[...], preferred_element_type=jnp.float32)
    mixed = mixed + weight_new * new_value_buf[...].astype(jnp.float32)
    attended = jnp.zeros((heads, HEAD_SIZE), jnp.float32)
    for b in range(kv_heads):
        attended = jnp.where(
            owner == b, mixed[:, b * HEAD_SIZE : (b + 1) * HEAD_SIZE], attended
        )
    attended = attended.astype(jnp.bfloat16).astype(jnp.float32)
    mine = residual_buf[...].astype(jnp.float32)
    rows = lax.broadcasted_iota(jnp.int32, mine.shape, 0)
    mine = jnp.sum(jnp.where(rows == sequence, mine, 0.0), axis=0, keepdims=True)
    out[...] = attended + head_rows(mine)

    count, tokens = id_buf.shape
    diagonal = lax.broadcasted_iota(jnp.int32, (tokens, tokens), 0) == lax.broadcasted_iota(
        jnp.int32, (tokens, tokens), 1
    )
    chosen = [as_column(id_buf[k : k + 1, :], diagonal) for k in range(count)]
    logit = [as_column(logit_buf[k : k + 1, :], diagonal) for k in range(count)]
    top = functools.reduce(jnp.maximum, logit)
    raised = [jnp.exp(v - top) for v in logit]
    scale = 1.0 / functools.reduce(jnp.add, raised)
    expert = lax.broadcasted_iota(jnp.int32, weights_out.shape, 1)
    by_expert = jnp.zeros(weights_out.shape, jnp.float32)
    for k in range(count):
        by_expert = by_expert + jnp.where(chosen[k] == expert, raised[k] * scale, 0.0)
    weights_out[...] = by_expert


def attend(lengths, queries, key_rows, value_rows, new_keys, new_values, residual, ids, logits):
    half_columns = LOCAL_HEADS * HEAD_SIZE
    operands = [lengths, queries, key_rows, value_rows, new_keys, new_values, residual, ids.T, logits.T]
    return pl.pallas_call(
        attend_kernel,
        out_shape=(
            jax.ShapeDtypeStruct((LOCAL_HEADS, HEAD_SIZE), jnp.float32),
            jax.ShapeDtypeStruct((ids.shape[0], E), jnp.float32),
        ),
        in_specs=[HBM] * len(operands),
        out_specs=(VMEM, VMEM),
        scratch_shapes=[
            pltpu.SMEM(lengths.shape, jnp.int32),
            pltpu.VMEM(queries.shape, jnp.bfloat16),
            pltpu.VMEM(key_rows.shape[1:], jnp.bfloat16),
            pltpu.VMEM(value_rows.shape[1:], jnp.bfloat16),
            pltpu.VMEM(new_keys.shape, jnp.bfloat16),
            pltpu.VMEM(new_values.shape, jnp.bfloat16),
            pltpu.VMEM((residual.shape[0], half_columns), jnp.bfloat16),
            pltpu.VMEM(ids.shape[::-1], jnp.int32),
            pltpu.VMEM(logits.shape[::-1], jnp.float32),
            pltpu.SemaphoreType.DMA((len(operands),)),
        ],
        compiler_params=pltpu.CompilerParams(vmem_limit_bytes=4 * MIB),
        cost_estimate=UNTIL_ROWS,
        name="attend",
    )(*in_hbm(*operands))


def norm_kernel(mine, other, gain, out):
    heads = mine.shape[0]
    own = mine[...]
    square = jnp.sum(own * own + other[...] * other[...], axis=0, keepdims=True)
    square = jnp.sum(square, axis=1, keepdims=True)
    inverse = lax.rsqrt(square * (1.0 / (SHARING_DEVICES * heads * HEAD_SIZE)) + 1e-05)
    at = pl.ds(pl.multiple_of(lax.axis_index("half") * heads, 8), heads)
    normed = (own * inverse * gain[at, :]).astype(jnp.bfloat16)
    out[...] = jnp.broadcast_to(normed[None], out.shape)


def norm(mine, other, gain, devices):
    shape = (devices,) + mine.shape
    return pl.pallas_call(
        norm_kernel,
        out_shape=jax.ShapeDtypeStruct(shape, jnp.bfloat16),
        in_specs=[VMEM] * 3,
        out_specs=VMEM,
        compiler_params=pltpu.CompilerParams(vmem_limit_bytes=MIB + 2 * math.prod(shape)),
        name="norm",
    )(mine, other, gain.reshape(-1, HEAD_SIZE))


class Job:
    def __init__(self, rows, weight, before, after, after_rows):
        self.rows, self.weight, self.before, self.after = rows, weight, before, after
        self.after_rows = after_rows


def run_jobs(jobs, sums):
    steps = [(n, k) for n, job in enumerate(jobs) for k in range(0, job.rows.shape[1], MXU)]

    def push(i):
        n, k = steps[i]
        job = jobs[n]
        if k == 0:
            job.before()
        for m in range(2):
            tile = job.weight[k : k + MXU, m * MXU : (m + 1) * MXU]
            pltpu.matmul_push_rhs(tile, i % 2, m)

    pending = []

    def settle():
        while pending:
            n = pending.pop()
            jobs[n].after([pltpu.matmul_pop(sums[n % 2][m]) for m in range(2)])

    push(0)
    for i, (n, k) in enumerate(steps):
        if i + 1 < len(steps):
            push(i + 1)
        job = jobs[n]
        if k == 0 and job.after_rows:
            settle()
        for m in range(2):
            pltpu.matmul_acc_lhs(sums[n % 2][m], job.rows[:, k : k + MXU], load_staged_rhs=i % 2)
        settle()
        if k + MXU == job.rows.shape[1]:
            pending.append(n)
    settle()


def experts_kernel(
    parts, w_gate, w_up, w_down, out, flat, normed, hidden, gates, total, ring, sems
):
    tokens, width = normed.shape
    slots, units = ring.shape[:2]
    heads = width // HEAD_SIZE
    group_rows, columns = out.shape[1:]
    targets = width // columns
    blocks = width // DOWN

    def down_copy(i):
        which, n = divmod(i, blocks)
        source = w_down.at[pl.ds(which * units, units), pl.ds(n * DOWN, DOWN)]
        return pltpu.make_async_copy(source, ring.at[i % slots], sems.at[i % slots])

    for i in range(min(slots, PASSES * blocks)):
        down_copy(i).start()

    flat[: tokens * heads, :] = parts[...].astype(jnp.float32).reshape(tokens * heads, HEAD_SIZE)
    for j in range(heads):
        normed[:, j * HEAD_SIZE : (j + 1) * HEAD_SIZE] = flat[
            pl.ds(j, tokens, stride=heads), :
        ].astype(jnp.bfloat16)

    def nothing():
        pass

    def gate_done(start):
        def after(sums):
            for m in range(2):
                gates[:, m * MXU : (m + 1) * MXU] = sums[m]

        return after

    def up_done(start):
        def after(sums):
            for m in range(2):
                gate = gates[:, m * MXU : (m + 1) * MXU]
                at = slice(start + m * MXU, start + (m + 1) * MXU)
                hidden[:, at] = (gate / (1.0 + jnp.exp(-gate)) * sums[m]).astype(jnp.bfloat16)

        return after

    def down_done(which, i, start):
        def after(sums):
            for m in range(2):
                column = start + m * MXU
                part = sums[m]
                at = slice(column, column + MXU)
                if which > 0:
                    part = total[:, at] + part
                if which < PASSES - 1:
                    total[:, at] = part
                    continue
                target, place = divmod(column, columns)
                for g in range(tokens // group_rows):
                    out[g * targets + target, :, place : place + MXU] = part[
                        g * group_rows : (g + 1) * group_rows
                    ].astype(out.dtype)
            if (start + 2 * MXU) % DOWN == 0 and i + slots < PASSES * blocks:
                down_copy(i + slots).start()

        return after

    jobs = []
    for which in range(PASSES):
        for start in range(which * units, (which + 1) * units, 2 * MXU):
            at = pl.ds(start, 2 * MXU)
            jobs.append(Job(normed, w_gate.at[:, at], nothing, gate_done(start), False))
            jobs.append(Job(normed, w_up.at[:, at], nothing, up_done(start), False))
        mine = hidden.at[:, pl.ds(which * units, units)]
        for n in range(blocks):
            i = which * blocks + n
            for start in range(0, DOWN, 2 * MXU):
                jobs.append(
                    Job(
                        mine,
                        ring.at[i % slots, :, pl.ds(start, 2 * MXU)],
                        down_copy(i).wait if start == 0 else nothing,
                        down_done(which, i, n * DOWN + start),
                        n == 0 and start == 0,
                    )
                )

    pl.run_scoped(
        lambda a, b, c, d: run_jobs(jobs, [[a, b], [c, d]]),
        *[pltpu.ACC(m)((tokens, MXU), jnp.float32) for _ in range(2) for m in range(2)],
    )


def experts(parts, w_gate, w_up, w_down, group_rows, dev_count):
    devices = parts.shape[0]
    width, local_hidden = w_gate.shape
    tokens = devices // SHARING_DEVICES
    columns = width // dev_count
    units = local_hidden // PASSES
    return pl.pallas_call(
        experts_kernel,
        out_shape=pltpu.VMEM((devices, group_rows, columns), jnp.bfloat16),
        in_specs=[VMEM, VMEM, VMEM, HBM],
        out_specs=VMEM,
        scratch_shapes=[
            pltpu.VMEM(((tokens + 1) * width // HEAD_SIZE, HEAD_SIZE), jnp.float32),
            pltpu.VMEM((tokens, width), jnp.bfloat16),
            pltpu.VMEM((tokens, local_hidden), jnp.bfloat16),
            pltpu.VMEM((tokens, 2 * MXU), jnp.float32),
            pltpu.VMEM((tokens, width), jnp.float32),
            pltpu.VMEM((RING, units, DOWN), jnp.bfloat16),
            pltpu.SemaphoreType.DMA((RING,)),
        ],
        compiler_params=pltpu.CompilerParams(vmem_limit_bytes=RING * units * DOWN * 2 + 2 * MIB),
        name="experts",
    )(*in_vmem(parts, w_gate, w_up), *in_hbm(w_down))


def experts_plain(parts, w_gate, w_up, w_down, group_rows, dev_count):
    width = w_gate.shape[0]
    normed = parts.reshape(-1, width)
    gate = jnp.dot(normed, w_gate, preferred_element_type=jnp.float32)
    up = jnp.dot(normed, w_up, preferred_element_type=jnp.float32)
    hidden = (jax.nn.silu(gate) * up).astype(jnp.bfloat16)
    part = jnp.dot(hidden, w_down, preferred_element_type=jnp.float32).astype(jnp.bfloat16)
    part = part.reshape(-1, group_rows, dev_count, width // dev_count)
    return part.transpose(0, 2, 1, 3).reshape(-1, group_rows, width // dev_count)


def combine_kernel(per_expert, dev_count, parts, weights, out):
    shards = parts.shape[0] // dev_count
    weight = weights[...]
    total = jnp.zeros(out.shape, jnp.float32)
    for e in range(E):
        here = jnp.zeros(out.shape, jnp.float32)
        for g in range(shards):
            for c in range(per_expert):
                here = here + parts[g * dev_count + e * per_expert + c].astype(jnp.float32)
        total = total + weight[:, e : e + 1] * here
    out[...] = total.astype(out.dtype)


def combine(parts, weights, dev_count):
    return pl.pallas_call(
        functools.partial(combine_kernel, dev_count // E, dev_count),
        out_shape=jax.ShapeDtypeStruct(parts.shape[1:], jnp.bfloat16),
        in_specs=[VMEM] * 2,
        out_specs=VMEM,
        compiler_params=pltpu.CompilerParams(vmem_limit_bytes=24 * MIB),
        name="combine",
    )(*in_vmem(parts, weights))


def body(
    queries,
    cached_key_rows,
    cached_value_rows,
    incoming_keys,
    incoming_values,
    lengths,
    residual,
    norm_gain,
    expert_ids,
    route_logits,
    w_gate,
    w_up,
    w_down,
):
    dev_count = lax.axis_size("pair") * SHARING_DEVICES
    group_rows = residual.shape[0]
    summed, weights = attend(
        lengths, queries, cached_key_rows, cached_value_rows, incoming_keys, incoming_values,
        residual, expert_ids, route_logits,
    )
    other = lax.ppermute(summed, "half", [(0, 1), (1, 0)])
    sent = norm(summed, other, norm_gain, lax.axis_size("grp") * dev_count)
    rows = lax.all_to_all(sent, ("grp", "pair", "half"), 0, 0, tiled=True)
    whole_blocks = w_gate.shape[1] % (PASSES * TILE) == 0 and norm_gain.shape[0] // dev_count % PART == 0
    run_experts = experts if whole_blocks else experts_plain
    part = run_experts(rows, w_gate, w_up, w_down, group_rows, dev_count)
    got = lax.all_to_all(part, ("grp", "pair", "half"), 0, 0, tiled=True)
    return combine(got, weights, dev_count)


def solution(mesh):
    groups, dev_count = mesh.devices.shape
    split = jax.sharding.Mesh(
        mesh.devices.reshape(groups, dev_count // SHARING_DEVICES, SHARING_DEVICES),
        ("grp", "pair", "half"),
    )
    dev = ("pair", "half")
    rows = ("grp",) + dev
    shards = dev + ("grp",)
    return jax.shard_map(
        body,
        mesh=split,
        in_specs=(
            P(rows, None),
            P(rows, None, None),
            P(rows, None, None),
            P(rows, None),
            P(rows, None),
            P("grp"),
            P("grp", None),
            P(),
            P("grp", None),
            P("grp", None),
            P(None, shards),
            P(None, shards),
            P(shards, None),
        ),
        out_specs=P("grp", dev),
        check_vma=False,
    )
```

```python
import functools
import math

import jax
import jax.numpy as jnp
from jax import lax
from jax.experimental import pallas as pl
from jax.experimental.pallas import tpu as pltpu
from jax.sharding import PartitionSpec as P

QUERY_HEADS = 48
KEY_VALUE_HEADS = 8
HEAD_SIZE = 128
E = 8
SHARING_DEVICES = 2
GROUP_WIDTH = QUERY_HEADS // KEY_VALUE_HEADS
LOCAL_HEADS = QUERY_HEADS // SHARING_DEVICES
MIB = 2**20
VMEM = pl.BlockSpec(memory_space=pltpu.VMEM)
HBM = pl.BlockSpec(memory_space=pltpu.HBM)
MXU = 256
TILE = 512
PART = 256
RING = 6
PASSES = 2
DOWN = 1024
CACHE_PARTS = 4
UNTIL_ROWS = pl.CostEstimate(flops=40_000_000_000, bytes_accessed=0, transcendentals=0)


def in_hbm(*arrays):
    return [pltpu.with_memory_space_constraint(a, pltpu.HBM) for a in arrays]


def in_vmem(*arrays):
    return [pltpu.with_memory_space_constraint(a, pltpu.VMEM) for a in arrays]


def head_rows(row):
    heads = row.shape[1] // HEAD_SIZE
    return jnp.concatenate(
        [row[:, j * HEAD_SIZE : (j + 1) * HEAD_SIZE] for j in range(heads)], axis=0
    )


def as_column(row, diagonal):
    return jnp.sum(jnp.where(diagonal, row, jnp.zeros_like(row)), axis=1, keepdims=True)


def attend_kernel(
    lengths, queries, key_rows, value_rows, new_keys, new_values, residual, ids, logits, out, weights_out,
    length_buf, query_buf, key_buf, value_buf, new_key_buf, new_value_buf, residual_buf, id_buf, logit_buf,
    sems,
):
    sequence, half = lax.axis_index("pair"), lax.axis_index("half")
    heads = LOCAL_HEADS
    columns = heads * HEAD_SIZE
    at = pl.ds(pl.multiple_of(half * columns, HEAD_SIZE), columns)
    pairs = [
        (queries, query_buf),
        (new_keys, new_key_buf),
        (lengths, length_buf),
        (new_values, new_value_buf),
        (residual.at[:, at], residual_buf),
        (ids, id_buf),
        (logits, logit_buf),
    ]
    copies = [pltpu.make_async_copy(*pair, sems.at[i]) for i, pair in enumerate(pairs)]
    cache_len, width = key_buf.shape
    step = cache_len // CACHE_PARTS

    def cache_copies(source, target, first):
        return [
            pltpu.make_async_copy(
                source.at[0, pl.ds(k * step, step)], target.at[pl.ds(k * step, step)], sems.at[first + k]
            )
            for k in range(CACHE_PARTS)
        ]

    key_copies = cache_copies(key_rows, key_buf, len(copies))
    value_copies = cache_copies(value_rows, value_buf, len(copies) + CACHE_PARTS)
    for copy in key_copies + copies + value_copies:
        copy.start()
    kv_heads = width // HEAD_SIZE
    scale = HEAD_SIZE ** (-0.5)
    for copy in key_copies + copies[:3]:
        copy.wait()
    query = head_rows(query_buf[...].astype(jnp.float32))
    owner = lax.broadcasted_iota(jnp.int32, (heads, HEAD_SIZE), 0) // GROUP_WIDTH
    blocks = [jnp.where(owner == b, query, 0.0) for b in range(kv_heads)]
    spread = jnp.concatenate(blocks, axis=1)
    scores = (
        lax.dot_general(
            spread.astype(jnp.bfloat16),
            key_buf[...],
            (((1,), (1,)), ((), ())),
            preferred_element_type=jnp.float32,
        )
        * scale
    )
    places = lax.broadcasted_iota(jnp.int32, (heads, cache_len), 1)
    scores = jnp.where(places < length_buf[sequence], scores, -1e30)
    new_score = (
        jnp.sum(spread * new_key_buf[...].astype(jnp.float32), axis=1, keepdims=True) * scale
    )
    row_max = jnp.maximum(jnp.max(scores, axis=1, keepdims=True), new_score)
    exp_all = jnp.exp(scores - row_max)
    exp_new = jnp.exp(new_score - row_max)
    denom = jnp.sum(exp_all, axis=1, keepdims=True) + exp_new
    weights = (exp_all / denom).astype(jnp.bfloat16)
    weight_new = (exp_new / denom).astype(jnp.bfloat16).astype(jnp.float32)
    for copy in copies[3:] + value_copies:
        copy.wait()
    mixed = jnp.dot(weights, value_buf[...], preferred_element_type=jnp.float32)
    mixed = mixed + weight_new * new_value_buf[...].astype(jnp.float32)
    attended = jnp.zeros((heads, HEAD_SIZE), jnp.float32)
    for b in range(kv_heads):
        attended = jnp.where(
            owner == b, mixed[:, b * HEAD_SIZE : (b + 1) * HEAD_SIZE], attended
        )
    attended = attended.astype(jnp.bfloat16).astype(jnp.float32)
    mine = residual_buf[...].astype(jnp.float32)
    rows = lax.broadcasted_iota(jnp.int32, mine.shape, 0)
    mine = jnp.sum(jnp.where(rows == sequence, mine, 0.0), axis=0, keepdims=True)
    out[...] = attended + head_rows(mine)

    count, tokens = id_buf.shape
    diagonal = lax.broadcasted_iota(jnp.int32, (tokens, tokens), 0) == lax.broadcasted_iota(
        jnp.int32, (tokens, tokens), 1
    )
    chosen = [as_column(id_buf[k : k + 1, :], diagonal) for k in range(count)]
    logit = [as_column(logit_buf[k : k + 1, :], diagonal) for k in range(count)]
    top = functools.reduce(jnp.maximum, logit)
    raised = [jnp.exp(v - top) for v in logit]
    scale = 1.0 / functools.reduce(jnp.add, raised)
    expert = lax.broadcasted_iota(jnp.int32, weights_out.shape, 1)
    by_expert = jnp.zeros(weights_out.shape, jnp.float32)
    for k in range(count):
        by_expert = by_expert + jnp.where(chosen[k] == expert, raised[k] * scale, 0.0)
    weights_out[...] = by_expert


def attend(lengths, queries, key_rows, value_rows, new_keys, new_values, residual, ids, logits):
    half_columns = LOCAL_HEADS * HEAD_SIZE
    operands = [lengths, queries, key_rows, value_rows, new_keys, new_values, residual, ids.T, logits.T]
    return pl.pallas_call(
        attend_kernel,
        out_shape=(
            jax.ShapeDtypeStruct((LOCAL_HEADS, HEAD_SIZE), jnp.float32),
            jax.ShapeDtypeStruct((ids.shape[0], E), jnp.float32),
        ),
        in_specs=[HBM] * len(operands),
        out_specs=(VMEM, VMEM),
        scratch_shapes=[
            pltpu.SMEM(lengths.shape, jnp.int32),
            pltpu.VMEM(queries.shape, jnp.bfloat16),
            pltpu.VMEM(key_rows.shape[1:], jnp.bfloat16),
            pltpu.VMEM(value_rows.shape[1:], jnp.bfloat16),
            pltpu.VMEM(new_keys.shape, jnp.bfloat16),
            pltpu.VMEM(new_values.shape, jnp.bfloat16),
            pltpu.VMEM((residual.shape[0], half_columns), jnp.bfloat16),
            pltpu.VMEM(ids.shape[::-1], jnp.int32),
            pltpu.VMEM(logits.shape[::-1], jnp.float32),
            pltpu.SemaphoreType.DMA((len(operands) - 2 + 2 * CACHE_PARTS,)),
        ],
        compiler_params=pltpu.CompilerParams(vmem_limit_bytes=4 * MIB),
        cost_estimate=UNTIL_ROWS,
        name="attend",
    )(*in_hbm(*operands))


def norm_kernel(mine, other, gain, out):
    heads = mine.shape[0]
    own = mine[...]
    square = jnp.sum(own * own + other[...] * other[...], axis=0, keepdims=True)
    square = jnp.sum(square, axis=1, keepdims=True)
    inverse = lax.rsqrt(square * (1.0 / (SHARING_DEVICES * heads * HEAD_SIZE)) + 1e-05)
    at = pl.ds(pl.multiple_of(lax.axis_index("half") * heads, 8), heads)
    normed = (own * inverse * gain[at, :]).astype(jnp.bfloat16)
    out[...] = jnp.broadcast_to(normed[None], out.shape)


def norm(mine, other, gain, devices):
    shape = (devices,) + mine.shape
    return pl.pallas_call(
        norm_kernel,
        out_shape=jax.ShapeDtypeStruct(shape, jnp.bfloat16),
        in_specs=[VMEM] * 3,
        out_specs=VMEM,
        compiler_params=pltpu.CompilerParams(vmem_limit_bytes=MIB + 2 * math.prod(shape)),
        name="norm",
    )(mine, other, gain.reshape(-1, HEAD_SIZE))


class Job:
    def __init__(self, rows, weight, before, after, after_rows):
        self.rows, self.weight, self.before, self.after = rows, weight, before, after
        self.after_rows = after_rows


def run_jobs(jobs, sums):
    steps = [(n, k) for n, job in enumerate(jobs) for k in range(0, job.rows.shape[1], MXU)]

    def push(i):
        n, k = steps[i]
        job = jobs[n]
        if k == 0:
            job.before()
        for m in range(2):
            tile = job.weight[k : k + MXU, m * MXU : (m + 1) * MXU]
            pltpu.matmul_push_rhs(tile, i % 2, m)

    pending = []

    def settle():
        while pending:
            n = pending.pop()
            jobs[n].after([pltpu.matmul_pop(sums[n % 2][m]) for m in range(2)])

    push(0)
    for i, (n, k) in enumerate(steps):
        if i + 1 < len(steps):
            push(i + 1)
        job = jobs[n]
        if k == 0 and job.after_rows:
            settle()
        for m in range(2):
            pltpu.matmul_acc_lhs(sums[n % 2][m], job.rows[:, k : k + MXU], load_staged_rhs=i % 2)
        settle()
        if k + MXU == job.rows.shape[1]:
            pending.append(n)
    settle()


def experts_kernel(
    parts, w_gate, w_up, w_down, out, flat, normed, hidden, gates, total, ring, sems
):
    tokens, width = normed.shape
    slots, units = ring.shape[:2]
    heads = width // HEAD_SIZE
    group_rows, columns = out.shape[1:]
    targets = width // columns
    blocks = width // DOWN

    def down_copy(i):
        which, n = divmod(i, blocks)
        source = w_down.at[pl.ds(which * units, units), pl.ds(n * DOWN, DOWN)]
        return pltpu.make_async_copy(source, ring.at[i % slots], sems.at[i % slots])

    for i in range(min(slots, PASSES * blocks)):
        down_copy(i).start()

    flat[: tokens * heads, :] = parts[...].astype(jnp.float32).reshape(tokens * heads, HEAD_SIZE)
    for j in range(heads):
        normed[:, j * HEAD_SIZE : (j + 1) * HEAD_SIZE] = flat[
            pl.ds(j, tokens, stride=heads), :
        ].astype(jnp.bfloat16)

    def nothing():
        pass

    def gate_done(start):
        def after(sums):
            for m in range(2):
                gates[:, m * MXU : (m + 1) * MXU] = sums[m]

        return after

    def up_done(start):
        def after(sums):
            for m in range(2):
                gate = gates[:, m * MXU : (m + 1) * MXU]
                at = slice(start + m * MXU, start + (m + 1) * MXU)
                hidden[:, at] = (gate / (1.0 + jnp.exp(-gate)) * sums[m]).astype(jnp.bfloat16)

        return after

    def down_done(which, i, start):
        def after(sums):
            for m in range(2):
                column = start + m * MXU
                part = sums[m]
                at = slice(column, column + MXU)
                if which > 0:
                    part = total[:, at] + part
                if which < PASSES - 1:
                    total[:, at] = part
                    continue
                target, place = divmod(column, columns)
                for g in range(tokens // group_rows):
                    out[g * targets + target, :, place : place + MXU] = part[
                        g * group_rows : (g + 1) * group_rows
                    ].astype(out.dtype)
            if (start + 2 * MXU) % DOWN == 0 and i + slots < PASSES * blocks:
                down_copy(i + slots).start()

        return after

    jobs = []
    for which in range(PASSES):
        for start in range(which * units, (which + 1) * units, 2 * MXU):
            at = pl.ds(start, 2 * MXU)
            jobs.append(Job(normed, w_gate.at[:, at], nothing, gate_done(start), False))
            jobs.append(Job(normed, w_up.at[:, at], nothing, up_done(start), False))
        mine = hidden.at[:, pl.ds(which * units, units)]
        for n in range(blocks):
            i = which * blocks + n
            for start in range(0, DOWN, 2 * MXU):
                jobs.append(
                    Job(
                        mine,
                        ring.at[i % slots, :, pl.ds(start, 2 * MXU)],
                        down_copy(i).wait if start == 0 else nothing,
                        down_done(which, i, n * DOWN + start),
                        n == 0 and start == 0,
                    )
                )

    pl.run_scoped(
        lambda a, b, c, d: run_jobs(jobs, [[a, b], [c, d]]),
        *[pltpu.ACC(m)((tokens, MXU), jnp.float32) for _ in range(2) for m in range(2)],
    )


def experts(parts, w_gate, w_up, w_down, group_rows, dev_count):
    devices = parts.shape[0]
    width, local_hidden = w_gate.shape
    tokens = devices // SHARING_DEVICES
    columns = width // dev_count
    units = local_hidden // PASSES
    return pl.pallas_call(
        experts_kernel,
        out_shape=pltpu.VMEM((devices, group_rows, columns), jnp.bfloat16),
        in_specs=[VMEM, VMEM, VMEM, HBM],
        out_specs=VMEM,
        scratch_shapes=[
            pltpu.VMEM(((tokens + 1) * width // HEAD_SIZE, HEAD_SIZE), jnp.float32),
            pltpu.VMEM((tokens, width), jnp.bfloat16),
            pltpu.VMEM((tokens, local_hidden), jnp.bfloat16),
            pltpu.VMEM((tokens, 2 * MXU), jnp.float32),
            pltpu.VMEM((tokens, width), jnp.float32),
            pltpu.VMEM((RING, units, DOWN), jnp.bfloat16),
            pltpu.SemaphoreType.DMA((RING,)),
        ],
        compiler_params=pltpu.CompilerParams(vmem_limit_bytes=RING * units * DOWN * 2 + 2 * MIB),
        name="experts",
    )(*in_vmem(parts, w_gate, w_up), *in_hbm(w_down))


def experts_plain(parts, w_gate, w_up, w_down, group_rows, dev_count):
    width = w_gate.shape[0]
    normed = parts.reshape(-1, width)
    gate = jnp.dot(normed, w_gate, preferred_element_type=jnp.float32)
    up = jnp.dot(normed, w_up, preferred_element_type=jnp.float32)
    hidden = (jax.nn.silu(gate) * up).astype(jnp.bfloat16)
    part = jnp.dot(hidden, w_down, preferred_element_type=jnp.float32).astype(jnp.bfloat16)
    part = part.reshape(-1, group_rows, dev_count, width // dev_count)
    return part.transpose(0, 2, 1, 3).reshape(-1, group_rows, width // dev_count)


def combine_kernel(per_expert, dev_count, parts, weights, out):
    shards = parts.shape[0] // dev_count
    weight = weights[...]
    total = jnp.zeros(out.shape, jnp.float32)
    for e in range(E):
        here = jnp.zeros(out.shape, jnp.float32)
        for g in range(shards):
            for c in range(per_expert):
                here = here + parts[g * dev_count + e * per_expert + c].astype(jnp.float32)
        total = total + weight[:, e : e + 1] * here
    out[...] = total.astype(out.dtype)


def combine(parts, weights, dev_count):
    return pl.pallas_call(
        functools.partial(combine_kernel, dev_count // E, dev_count),
        out_shape=jax.ShapeDtypeStruct(parts.shape[1:], jnp.bfloat16),
        in_specs=[VMEM] * 2,
        out_specs=VMEM,
        compiler_params=pltpu.CompilerParams(vmem_limit_bytes=24 * MIB),
        name="combine",
    )(*in_vmem(parts, weights))


def body(
    queries,
    cached_key_rows,
    cached_value_rows,
    incoming_keys,
    incoming_values,
    lengths,
    residual,
    norm_gain,
    expert_ids,
    route_logits,
    w_gate,
    w_up,
    w_down,
):
    dev_count = lax.axis_size("pair") * SHARING_DEVICES
    group_rows = residual.shape[0]
    summed, weights = attend(
        lengths, queries, cached_key_rows, cached_value_rows, incoming_keys, incoming_values,
        residual, expert_ids, route_logits,
    )
    other = lax.ppermute(summed, "half", [(0, 1), (1, 0)])
    sent = norm(summed, other, norm_gain, lax.axis_size("grp") * dev_count)
    rows = lax.all_to_all(sent, ("grp", "pair", "half"), 0, 0, tiled=True)
    whole_blocks = w_gate.shape[1] % (PASSES * TILE) == 0 and norm_gain.shape[0] // dev_count % PART == 0
    run_experts = experts if whole_blocks else experts_plain
    part = run_experts(rows, w_gate, w_up, w_down, group_rows, dev_count)
    got = lax.all_to_all(part, ("grp", "pair", "half"), 0, 0, tiled=True)
    return combine(got, weights, dev_count)


def solution(mesh):
    groups, dev_count = mesh.devices.shape
    split = jax.sharding.Mesh(
        mesh.devices.reshape(groups, dev_count // SHARING_DEVICES, SHARING_DEVICES),
        ("grp", "pair", "half"),
    )
    dev = ("pair", "half")
    rows = ("grp",) + dev
    shards = dev + ("grp",)
    return jax.shard_map(
        body,
        mesh=split,
        in_specs=(
            P(rows, None),
            P(rows, None, None),
            P(rows, None, None),
            P(rows, None),
            P(rows, None),
            P("grp"),
            P("grp", None),
            P(),
            P("grp", None),
            P("grp", None),
            P(None, shards),
            P(None, shards),
            P(shards, None),
        ),
        out_specs=P("grp", dev),
        check_vma=False,
    )
```
